128 devices in a mesh: tile: 32 (over y, x, core), knot: 4 (over z).
Axes of the slice: x: 4, y: 4, z: 4, core: 2. Of those that a mesh axis runs over, the one named last changes fastest.
Arguments:
- images: float32 [32, 32, 65536], P('tile', 'knot'), may hold values from -6 to 6
- gradient: float32 [32, 32, 65536], P('tile', 'knot'), may hold values from -3 to 3
- shifts: int32 [32], P('tile'), may hold values from -4 to 4
- tile_blocks: int32 [32, 2], P('tile'), may hold values from 0 to 127, as said below
- intersections: int32 [32, 3, 8, 5], P('tile'), may hold values from 0 to 57344, as said below
- start_coefficients: float32 [128, 64], P(('tile', 'knot')), may hold values from -0.6 to 0.6
Outputs:
- coefficients: float32 [128, 64], P(('tile', 'knot'))
- warped: float32 [32, 32, 65536], P('tile', 'knot')
The draws below stay inside these ranges and needn't reach their ends.
Inputs may be any that keep to these rules, and one draw needn't show every extreme that they name: intersections[s, d, m] holds the sending tile's index among the 1 tiles of owner s, its slab offset, the receiving tile's index among the tiles of owner s + d - 1, its slab offset, and a live flag; live slots of one sender and direction come first; no live slot points outside the owners; some owner receives 8 live slots from each of its three senders, and some sender fills 8 slots of a direction. `tile_blocks`: the blocks of a tile held by tile owner i are owned by tile owners i - 1, i or i + 1, block b being owned by device b div 1 in the order of tile and knot joined.
All inputs are finite; a program needn't handle non-finite values.
Results may differ from the reference program's by a relative error of at most 0.0003.
Values sent between devices are 32-bit elements; how exact they have to be, the bound alone decides.
No kernel may reach another device: no remote copies, remote signals or barrier semaphores. Data moves between devices by JAX's collectives and lax.ppermute only.
A program may use at most 576 MiB of HBM per device.

```python
import jax
import jax.numpy as jnp
from jax import lax

TILE_DEV = 1
PLANE = 65536
SLAB = 8192
CAP = 8
BLOCK = 64
ITERS = 2
TILES = 32
Z = 32
KNOT_BLOCKS = 128


def draw_tile_blocks(key, part):
    key = jax.random.fold_in(key, 11)
    owners = TILES // TILE_DEV
    width = KNOT_BLOCKS // owners
    home = jnp.arange(TILES, dtype=jnp.int32) // TILE_DEV
    low = jnp.maximum(home - 1, 0) * width
    high = jnp.minimum(home + 2, owners) * width
    picked = jax.random.randint(key, (TILES, 2), low[:, None], high[:, None], dtype=jnp.int32)
    picked = picked.at[0, 0].set(0)
    return picked.at[TILES - 1, 1].set(KNOT_BLOCKS - 1)


def draw_intersections(key, part):
    key = jax.random.fold_in(key, 23)
    owners = TILES // TILE_DEV
    keys = jax.random.split(key, 6)
    shape = (owners, 3, CAP)
    src_tile = jax.random.randint(keys[0], shape, 0, TILE_DEV, dtype=jnp.int32)
    src_off = jax.random.randint(keys[1], shape, 0, PLANE - SLAB + 1, dtype=jnp.int32)
    dst_tile = jax.random.randint(keys[2], shape, 0, TILE_DEV, dtype=jnp.int32)
    dst_off = jax.random.randint(keys[3], shape, 0, PLANE - SLAB + 1, dtype=jnp.int32)
    src_off = src_off.at[0, 1, 0].set(PLANE - SLAB)
    count = jax.random.randint(keys[4], (owners, 3), 1, CAP + 1, dtype=jnp.int32)
    chosen = jax.random.randint(keys[5], (), 1, owners - 1, dtype=jnp.int32)
    rows = jnp.arange(owners, dtype=jnp.int32)[:, None]
    dirs = jnp.arange(3, dtype=jnp.int32)[None, :]
    target = rows + dirs - 1
    count = jnp.where(target == chosen, CAP, count)
    count = jnp.where((target < 0) | (target >= owners), 0, count)
    live = (jnp.arange(CAP, dtype=jnp.int32)[None, None, :] < count[:, :, None]).astype(jnp.int32)
    return jnp.stack([src_tile, src_off, dst_tile, dst_off, live], axis=-1)


def plant(array, own_key, low, top_value):
    longest = array.shape.index(max(array.shape))
    spots = []
    for shift in (0, 1):
        where = [jax.random.randint(jax.random.fold_in(own_key, axis), (), 0, length) for axis, length in enumerate(array.shape)]
        where[longest] = (where[longest] + shift) % array.shape[longest]
        spots.append(tuple(where))
    return array.at[spots[0]].set(low).at[spots[1]].set(top_value)


def shard_levels(stream_key, shape, pieces, least, high):
    def one(dim, shards_of):
        steps = jax.random.uniform(jax.random.fold_in(jax.random.fold_in(stream_key, 6), dim), (shards_of,), jnp.float32, least / len(pieces), high / len(pieces))
        return jnp.repeat(jnp.exp(steps), shape[dim] // shards_of).reshape((-1,) + (1,) * (len(shape) - dim - 1))

    factor_of = one(*pieces[0])
    for cut in pieces[1:]:
        factor_of = factor_of * one(*cut)
    return factor_of


def noise(key, dims, scale, reach, pieces=(), kind=jnp.bfloat16):
    gain = shard_levels(key, dims, pieces, -0.22, 0.18) if pieces else 1.0
    result = jax.random.normal(key, dims, jnp.float32) * scale * gain
    return jnp.minimum(jnp.maximum(result, -reach), reach).astype(kind)


def setup_inputs(seed: int = 0) -> dict:
    seeds = jax.random.split(jax.random.key(seed), 7)
    images = noise(seeds[0], (TILES, Z, PLANE), 1.0, 6.0, ((0, 32), (1, 4)), jnp.float32)
    gradient = noise(seeds[1], (TILES, Z, PLANE), 0.5, 3.0, ((0, 32), (1, 4)), jnp.float32)
    shifts = plant(jax.random.randint(seeds[2], (TILES,), -4, 5), jax.random.fold_in(seeds[2], 1), -4, 4).astype(jnp.int32)
    tile_blocks = draw_tile_blocks(jax.random.fold_in(seeds[6], 71), 0)
    intersections = draw_intersections(jax.random.fold_in(seeds[6], 71), 0)
    start_coefficients = noise(seeds[5], (KNOT_BLOCKS, BLOCK), 0.1, 0.6, ((0, 128),), jnp.float32)
    return dict(images=images, gradient=gradient, shifts=shifts, tile_blocks=tile_blocks, intersections=intersections, start_coefficients=start_coefficients)


shift_step = 0.05
smooth_weight = 20.0
ridge_weight = 1.0

def spline_basis(plane, knots):
    place = jnp.arange(plane, dtype=jnp.float32) * ((knots - 3) / plane) + 1.0
    offset = place[None, :] - jnp.arange(knots, dtype=jnp.float32)[:, None]
    dist = jnp.abs(offset)
    inner = 2.0 / 3.0 - dist * dist + 0.5 * dist * dist * dist
    outer = (2.0 - dist) * (2.0 - dist) * (2.0 - dist) / 6.0
    return jnp.where(dist < 1.0, inner, jnp.where(dist < 2.0, outer, 0.0))

def smoothing(block):
    rows = jnp.arange(block - 2, dtype=jnp.int32)[:, None]
    cols = jnp.arange(block, dtype=jnp.int32)[None, :]
    second = (cols == rows).astype(jnp.float32) - 2.0 * (cols == rows + 1).astype(jnp.float32) + (cols == rows + 2).astype(jnp.float32)
    return jnp.dot(second.T, second, precision=lax.Precision.HIGHEST)

def block_update(normal, gradsum, coef, penalty):
    size = normal.shape[-1]
    system = normal + smooth_weight * penalty + ridge_weight * jnp.eye(size, dtype=jnp.float32)
    pull = jnp.einsum('kl,bl->bk', penalty, coef, precision=lax.Precision.HIGHEST)
    target = -(gradsum + smooth_weight * pull)
    factor = lax.linalg.cholesky(system)
    middle = lax.linalg.triangular_solve(factor, target[..., None], left_side=True, lower=True)
    update = lax.linalg.triangular_solve(factor, middle, left_side=True, lower=True, transpose_a=True)
    return coef + update[..., 0]

def warp_tiles(images, gradient, shifts, tile_blocks, coef, basis):
    local = coef[tile_blocks].reshape(tile_blocks.shape[0], -1)
    field = jnp.dot(local, basis, precision=lax.Precision.HIGHEST)
    offset = field + shift_step * shifts.astype(jnp.float32)[:, None]
    return images + gradient * offset[:, None, :]

def reference(images, gradient, shifts, tile_blocks, intersections, start_coefficients):
    basis = spline_basis(PLANE, 2 * BLOCK)
    penalty = smoothing(BLOCK)
    senders = intersections.shape[0]
    source = jnp.arange(senders, dtype=jnp.int32)[:, None, None]
    receiver = jnp.clip(source + jnp.arange(3, dtype=jnp.int32)[None, :, None] - 1, 0, senders - 1)
    tile_b = (source * TILE_DEV + intersections[..., 0]).reshape(-1).astype(jnp.int32)
    off_b = intersections[..., 1].reshape(-1).astype(jnp.int32)
    tile_a = (receiver * TILE_DEV + intersections[..., 2]).reshape(-1).astype(jnp.int32)
    off_a = intersections[..., 3].reshape(-1).astype(jnp.int32)
    alive = intersections[..., 4].reshape(-1).astype(jnp.float32)
    zero = jnp.zeros((), jnp.int32)
    targets = tile_blocks[tile_a].reshape(-1)
    coef = start_coefficients
    for step in range(ITERS):
        tiles = warp_tiles(images, gradient, shifts, tile_blocks, coef, basis)

        def pair_terms(item):
            tb, ob, ta, oa, live = item
            far = lax.dynamic_slice(tiles, (tb, zero, ob), (1, Z, SLAB))[0]
            near = lax.dynamic_slice(tiles, (ta, zero, oa), (1, Z, SLAB))[0]
            slope = lax.dynamic_slice(gradient, (ta, zero, oa), (1, Z, SLAB))[0]
            misfit = (near - far) * live
            weight = jnp.sum(slope * slope, axis=0) * live
            project = jnp.sum(slope * misfit, axis=0)
            piece = lax.dynamic_slice(basis, (zero, oa), (2 * BLOCK, SLAB)).reshape(2, BLOCK, SLAB)
            normal = jnp.einsum('nks,nls->nkl', piece * weight[None, None, :], piece, precision=lax.Precision.HIGHEST)
            grads = jnp.einsum('nks,s->nk', piece, project, precision=lax.Precision.HIGHEST)
            return (normal, grads)
        normals, grads = lax.map(pair_terms, (tile_b, off_b, tile_a, off_a, alive))
        normal_sum = jnp.zeros((KNOT_BLOCKS, BLOCK, BLOCK), jnp.float32).at[targets].add(normals.reshape(-1, BLOCK, BLOCK))
        grad_sum = jnp.zeros((KNOT_BLOCKS, BLOCK), jnp.float32).at[targets].add(grads.reshape(-1, BLOCK))
        coef = block_update(normal_sum, grad_sum, coef, penalty)
    warped = warp_tiles(images, gradient, shifts, tile_blocks, coef, basis)
    return (coef, warped)
```

```python
import functools

import jax
import jax.numpy as jnp
from jax import lax
from jax.experimental import pallas as pl
from jax.experimental.pallas import tpu as pltpu
from jax.sharding import PartitionSpec as P

SLAB = 8192
BLOCK = 64
LANES = 128
ROWS = 512
DEPTH = 8
LEAD = 8
PADDED = LEAD + ROWS + 16
GROUPS = SLAB // (8 * LANES) + 1
SLAB_ROWS = 8 * GROUPS
CAP = 8

shift_step = 0.05
smooth_weight = 20.0
ridge_weight = 1.0

EXACT = lax.Precision.HIGHEST
VMEM_LIMIT = 48 * 1024 * 1024


def iota(shape, dim):
    return lax.broadcasted_iota(jnp.int32, shape, dim)


def dot(a, b):
    return lax.dot_general(
        a, b, (((1,), (0,)), ((), ())), precision=EXACT, preferred_element_type=jnp.float32
    )


def dot_rows(a, b):
    return lax.dot_general(
        a, b, (((1,), (1,)), ((), ())), precision=EXACT, preferred_element_type=jnp.float32
    )


class Spline:
    def __init__(self):
        row = iota((ROWS, LANES), 0)
        lane = iota((ROWS, LANES), 1)
        self.low = (((row * LANES + lane) * 125) >> 16) == ((row * 125) >> 9)
        self.hot = (lane == ((row * 125) >> 9)).astype(jnp.float32)
        sub = iota((8, ROWS), 0)
        col = iota((8, ROWS), 1)
        first = (col * 125) >> 9
        centre = ((col * 256 + 127) * 125).astype(jnp.float32) * (1.0 / 131072.0)
        u = centre - first.astype(jnp.float32) - (sub >= 4).astype(jnp.float32)
        t = 1.0 - u
        k = 64.0 * 125.0 / 65536.0
        which = sub & 3
        def pick(a, b, c, d):
            return jnp.where(which == 0, a, jnp.where(which == 1, b, jnp.where(which == 2, c, d)))
        self.cubic = [
            pick(
                t * t * t / 6.0,
                2.0 / 3.0 - u * u + 0.5 * u * u * u,
                2.0 / 3.0 - t * t + 0.5 * t * t * t,
                u * u * u / 6.0,
            ),
            k * pick(-0.5 * t * t, -2.0 * u + 1.5 * u * u, 2.0 * t - 1.5 * t * t, 0.5 * u * u),
            (k * k) * pick(0.5 * t, 1.5 * u - 1.0, 1.5 * t - 1.0, 0.5 * u),
            (k * k * k) * pick(-1.0 / 6.0, 0.5, -0.5, 1.0 / 6.0),
        ]
        self.sub = sub
        eta = (iota((8, LANES), 1).astype(jnp.float32) - 63.5) * (1.0 / 64.0)
        power = iota((8, LANES), 0)
        q = jnp.ones((8, LANES), jnp.float32)
        for n in range(7):
            q = jnp.where(power > n, q * eta, q)
        self.powers = q

    def field(self, local):
        rows = [pltpu.roll(local, (LANES - s) % LANES, 1) if s else local for s in (0, 1, 2, 3)]
        rows += [pltpu.roll(local, LANES - s, 1) for s in (1, 2, 3, 4)]
        near = dot_rows(jnp.concatenate(rows, axis=0), self.hot)
        terms = jnp.concatenate([c * near for c in self.cubic], axis=0)
        wide = iota((32, 2 * LANES), 1)
        high = (iota((32, 2 * LANES), 0) & 4) != 0
        order = iota((32, 2 * LANES), 0) >> 3
        eta = ((wide & 127).astype(jnp.float32) - 63.5) * (1.0 / 64.0)
        power = jnp.where(
            order == 0, 1.0, jnp.where(order == 1, eta, jnp.where(order == 2, eta * eta, eta * eta * eta))
        )
        power = jnp.where(high == (wide >= LANES), power, 0.0)
        both = dot(terms.T, power)
        return jnp.where(self.low, both[:, :LANES], both[:, LANES:])

    def moments(self, value):
        low = jnp.where(self.low, value, 0.0)
        high = jnp.where(self.low, 0.0, value)
        a = dot_rows(self.powers, low)
        b = dot_rows(self.powers, high)
        return lambda n: jnp.where(self.sub < 4, a[n : n + 1], b[n : n + 1])

    def gather(self, rows):
        total = rows[0:1]
        for s in range(1, 4):
            total = total + pltpu.roll(rows[s : s + 1], s, 1)
        for s in range(4):
            total = total + pltpu.roll(rows[4 + s : 5 + s], s + 1, 1)
        return total

    def adjoint(self, value):
        part = self.moments(value)
        rows = sum(self.cubic[n] * part(n) for n in range(4))
        return self.gather(dot(rows, self.hot))

    def band(self, value):
        part = self.moments(value)
        parts = [part(n) for n in range(7)]
        y = [sum(self.cubic[j] * parts[i + j] for j in range(4)) for i in range(4)]
        stack = []
        for m in range(4):
            moved = [pltpu.roll(v, 8 - m, 0) if m else v for v in y]
            rows = sum(self.cubic[i] * moved[i] for i in range(4))
            stack.append(jnp.where((self.sub & 3) + m < 4, rows, 0.0))
        rows = dot(jnp.concatenate(stack, axis=0), self.hot)
        return [self.gather(rows[8 * m : 8 * m + 8]) for m in range(4)]


def place(pair, p):
    off_b, off_a = pair(p, 1), pair(p, 3)
    row_b = off_b >> 7
    lead = off_b & 127
    start = off_a - lead
    row_a = start >> 7
    turn = start & 127
    return row_b, lead, row_a, turn


def add_moved(accs, row_a, turn, i, value):
    lane = iota((8, LANES), 1)
    moved = pltpu.roll(value, turn, 1)
    keep = lane >= turn
    at = pl.ds(row_a + (LEAD + 8 * i), 8)
    accs[0][at, :] += jnp.where(keep, moved, 0.0)
    accs[1][at, :] += jnp.where(keep, 0.0, moved)


def live_count(pair):
    total = pair(0, 4)
    for p in range(1, CAP):
        total = total + pair(p, 4)
    return total


def pair_reader(ref, direction):
    return lambda p, field: ref[(direction * CAP + p) * 5 + field]


def slabs(pair, base, far, grad, image, field, cross, accs):
    lane = iota((8, LANES), 1)
    sub = iota((8, LANES), 0)

    def body(p, carry):
        row_b, lead, row_a, turn = place(pair, p)
        back = (LANES - turn) & 127
        keep = lane >= turn
        for i in range(GROUPS):
            c = jnp.zeros((8, LANES), jnp.float32)
            x = jnp.zeros((8, LANES), jnp.float32)
            for z in range(DEPTH):
                at_a = (row_a + (LEAD + 8 * i)) * 8 + z
                at_b = (row_b + (LEAD + 8 * i)) * 8 + z
                first = far[pl.ds(at_a, 8, stride=8), :]
                second = far[pl.ds(at_a + 8, 8, stride=8), :]
                slope = pltpu.roll(jnp.where(keep, first, second), back, 1)
                c = c + slope * grad[pl.ds(at_b, 8, stride=8), :]
                x = x + slope * image[pl.ds(at_b, 8, stride=8), :]
            if i in (0, GROUPS - 1):
                s = (sub + 8 * i) * LANES + lane - lead
                valid = (s >= 0) & (s < SLAB)
                c = jnp.where(valid, c, 0.0)
                x = jnp.where(valid, x, 0.0)
            cross[base + p, 8 * i : 8 * i + 8, :] = c
            value = x + c * field[pl.ds(row_b + (LEAD + 8 * i), 8), :]
            add_moved(accs, row_a, turn, i, value)
        return carry

    lax.fori_loop(0, live_count(pair), body, 0)


def slab_steps(pair, base, field, cross, accs):
    def body(p, carry):
        row_b, lead, row_a, turn = place(pair, p)
        for i in range(GROUPS):
            c = cross[base + p, 8 * i : 8 * i + 8, :]
            value = c * field[pl.ds(row_b + (LEAD + 8 * i), 8), :]
            add_moved(accs, row_a, turn, i, value)
        return carry

    lax.fori_loop(0, live_count(pair), body, 0)


def collected(accs):
    return accs[0][LEAD : LEAD + ROWS, :] + accs[1][LEAD - 1 : LEAD + ROWS - 1, :]


def clear(refs):
    for ref in refs:
        ref[...] = jnp.zeros(ref.shape, jnp.float32)


def clear_ends(ref, step):
    ref[0 : LEAD * step, :] = jnp.zeros((LEAD * step, LANES), jnp.float32)
    ref[(LEAD + ROWS) * step :, :] = jnp.zeros(((PADDED - LEAD - ROWS) * step, LANES), jnp.float32)


def local_values(place_ref, own, side_a, side_b):
    here = place_ref[0]
    lane = iota((1, LANES), 1)
    out = []
    for n in range(2):
        block = place_ref[1 + n]
        col, slot = block >> 2, block & 3
        table = jnp.where(
            col == here, own[0:2, :], jnp.where(col == (here ^ 1), side_a[0:2, :], side_b[0:2, :])
        )
        row = jnp.where((slot >> 1) == 0, table[0:1], table[1:2])
        row = jnp.where((slot & 1) == 0, row, pltpu.roll(row, BLOCK, 1))
        out.append(row)
    return jnp.where(lane < BLOCK, out[0], pltpu.roll(out[1], BLOCK, 1))


def padded_copy(source, target, sem):
    return pltpu.make_async_copy(source, target.at[pl.ds(LEAD * 8, ROWS * 8)], sem)


def directions(place_ref):
    odd = place_ref[0] & 1
    return jnp.where(odd == 0, 2, 0), jnp.where(odd == 0, 0, 2)


def early_kernel(
    place_ref, meta_own, meta_a, meta_b, own, side_a, side_b, grad_in, image_in, far_in,
    cross, weight_out, field_out, part_out,
    grad, image, far, acc0, acc1, acc2, acc3, count, sems,
):
    copies = [
        padded_copy(s, t, sems.at[n])
        for n, (s, t) in enumerate(((grad_in, grad), (image_in, image), (far_in, far)))
    ]
    for c in copies:
        c.start()
    for ref in (grad, image, far):
        clear_ends(ref, 8)
    clear((acc0, acc1, acc2, acc3, count))
    clear_ends(field_out, 1)
    spline = Spline()
    local = local_values(place_ref, own, side_a, side_b)
    rigid = shift_step * place_ref[3].astype(jnp.float32)
    field_out[LEAD : LEAD + ROWS, :] = spline.field(local) + rigid

    dir_a, dir_b = directions(place_ref)
    lane = iota((8, LANES), 1)
    sub = iota((8, LANES), 0)

    def cover(pair):
        def body(p, carry):
            off = pair(p, 3)
            row = off >> 7
            for i in range(GROUPS):
                s = (sub + 8 * i) * LANES + lane - (off & 127)
                inside = (s >= 0) & (s < SLAB)
                count[pl.ds(row + (LEAD + 8 * i), 8), :] += jnp.where(inside, 1.0, 0.0)
            return carry

        lax.fori_loop(0, live_count(pair), body, 0)

    own_pairs = pair_reader(meta_own, 1)
    cover(own_pairs)
    cover(pair_reader(meta_a, 2 - dir_a))
    cover(pair_reader(meta_b, 2 - dir_b))
    for c in copies:
        c.wait()
    slabs(own_pairs, 0, grad, grad, image, field_out, cross, (acc0, acc1))
    slabs(pair_reader(meta_own, dir_a), CAP, far, grad, image, field_out, cross, (acc2, acc3))

    def rows(g, carry):
        w = jnp.zeros((8, LANES), jnp.float32)
        v = jnp.zeros((8, LANES), jnp.float32)
        for z in range(DEPTH):
            at = pl.ds((LEAD + 8 * g) * 8 + z, 8, stride=8)
            slope = grad[at, :]
            w = w + slope * slope
            v = v + slope * image[at, :]
        at = pl.ds(pl.multiple_of(LEAD + 8 * g, 8), 8)
        n = count[at, :]
        w = w * n
        weight_out[pl.ds(pl.multiple_of(8 * g, 8), 8), :] = w
        count[at, :] = v * n + w * field_out[at, :]
        return carry

    lax.fori_loop(0, ROWS // 8, rows, 0)
    part_out[0:1, :] = spline.adjoint(count[LEAD : LEAD + ROWS, :] - collected((acc0, acc1)))
    part_out[1:2, :] = -spline.adjoint(collected((acc2, acc3)))
    part_out[2:3, :] = jnp.zeros((1, LANES), jnp.float32)
    half = iota((1, LANES), 1) < BLOCK
    first = jnp.where(place_ref[4] == 0, 1.0, 0.0)
    part_out[3:4, :] = first * jnp.where(half, place_ref[1], place_ref[2]).astype(jnp.float32)
    for m, row in enumerate(spline.band(weight_out[...])):
        part_out[4 + m : 5 + m, :] = row


def late_kernel(
    place_ref, meta_own, field, part, grad_in, image_in, far_in,
    cross, part_out, grad, image, far, acc0, acc1, sems,
):
    copies = [
        padded_copy(s, t, sems.at[n])
        for n, (s, t) in enumerate(((grad_in, grad), (image_in, image), (far_in, far)))
    ]
    for c in copies:
        c.start()
    for ref in (grad, image, far):
        clear_ends(ref, 8)
    clear((acc0, acc1))
    spline = Spline()
    _, dir_b = directions(place_ref)
    for c in copies:
        c.wait()
    slabs(pair_reader(meta_own, dir_b), 0, far, grad, image, field, cross, (acc0, acc1))
    part_out[...] = part[...]
    part_out[2:3, :] = -spline.adjoint(collected((acc0, acc1)))


def block_ids(place_ref):
    return [
        place_ref[1].astype(jnp.float32),
        place_ref[2].astype(jnp.float32),
        (place_ref[0] * 4 + place_ref[4]).astype(jnp.float32),
    ]


def near_tiles(me, a, b, c, d, sb, sd):
    return [
        (me, me[0:1, :] + a[1:2, :] + b[2:3, :]),
        (a, a[0:1, :] + me[1:2, :] + sb[2:3, :]),
        (b, b[0:1, :] + d[1:2, :] + me[2:3, :]),
        (d, d[0:1, :] + b[1:2, :] + c[2:3, :]),
        (sb, sb[0:1, :] + sd[1:2, :] + a[2:3, :]),
    ]


def folded(rows):
    return rows + pltpu.roll(rows, BLOCK, 1)


def block_sums(tiles, block):
    total = jnp.zeros((1, LANES), jnp.float32)
    for ref, grad in tiles:
        total = total + jnp.where(ref[3:4, :] == block, grad, 0.0)
    lane = iota((1, LANES), 1)
    return jnp.where(lane < BLOCK, folded(total), 0.0)


def pulled(coef):
    lane = iota((1, LANES), 1)
    y = coef - 2.0 * pltpu.roll(coef, LANES - 1, 1) + pltpu.roll(coef, LANES - 2, 1)
    y = jnp.where(lane < BLOCK - 2, y, 0.0)
    return jnp.where(lane < BLOCK, y - 2.0 * pltpu.roll(y, 1, 1) + pltpu.roll(y, 2, 1), 0.0)


def solve(target, factor, steps):
    y = []
    for i in range(BLOCK):
        v = target[i : i + 1, :]
        for j in range(1, 4):
            if i >= j:
                v = v - factor[j * BLOCK + i - j : j * BLOCK + i - j + 1, :] * y[i - j]
        y.append(v)
    x = [None] * BLOCK
    for i in reversed(range(BLOCK)):
        v = y[i] * factor[i : i + 1, :]
        for j in range(3, 0, -1):
            if i + j < BLOCK:
                v = v - factor[j * BLOCK + i : j * BLOCK + i + 1, :] * x[i + j]
        x[i] = v
        steps[i : i + 1, :] = v


def across(rows):
    block = jnp.concatenate(rows + [jnp.zeros((LANES - len(rows), LANES), jnp.float32)], axis=0)
    return block.T


def joined(coefs):
    lane = iota((1, LANES), 1)
    return jnp.where(lane < BLOCK, coefs[0], pltpu.roll(coefs[1], BLOCK, 1))


def step_kernel(
    place_ref, meta_own, me, a, b, c, d, sb, sd, own, side_a, side_b, start, weight,
    cross_early, cross_late,
    part_out, state, factor,
    field, steps, work, acc0, acc1, acc2, acc3, acc4, acc5,
):
    clear((acc0, acc1, acc2, acc3, acc4, acc5, steps))
    clear_ends(field, 1)
    lane = iota((1, LANES), 1)
    zero = jnp.zeros((1, LANES), jnp.float32)
    tiles = near_tiles(me, a, b, c, d, sb, sd)
    both = local_values(place_ref, own, side_a, side_b)
    coefs = [
        jnp.where(lane < BLOCK, both, 0.0),
        jnp.where(lane < BLOCK, pltpu.roll(both, BLOCK, 1), 0.0),
        start[0:1, :],
    ]
    sums = []
    rows = []
    for q, block in enumerate(block_ids(place_ref)):
        gradsum = block_sums(tiles, block)
        sums.append(gradsum)
        bands = []
        for m in range(4):
            total = zero
            for ref, _ in tiles:
                total = total + jnp.where(ref[3:4, :] == block, ref[4 + m : 5 + m, :], 0.0)
            total = jnp.where((lane & (BLOCK - 1)) + m < BLOCK, total, 0.0)
            bands.append(folded(total))
        inside = lambda cond: jnp.where(cond, 1.0, 0.0)
        upper, lower = inside(lane < BLOCK - 2), inside(lane >= 2)
        middle = inside((lane >= 1) & (lane < BLOCK - 1))
        bands[0] = bands[0] + smooth_weight * (upper + 4.0 * middle + lower) + ridge_weight
        bands[1] = bands[1] - smooth_weight * 2.0 * (
            upper + inside((lane >= 1) & (lane < BLOCK - 1))
        )
        bands[2] = bands[2] + smooth_weight * upper
        target = -(gradsum + smooth_weight * pulled(coefs[q]))
        rows += bands + [target, zero, zero, zero]
    work[...] = across(rows)
    turned = [work[0:BLOCK, :]] + [pltpu.roll(work[0:BLOCK, :], LANES - m, 1) for m in range(1, 5)]
    band = [[turned[m][i : i + 1, :] for i in range(BLOCK)] for m in range(4)]
    for i in range(BLOCK):
        r = 1.0 / band[0][i]
        factor[i : i + 1, :] = r
        cs = [band[m][i] for m in range(1, 4)]
        ls = [v * r for v in cs]
        for j in range(1, 4):
            factor[j * BLOCK + i : j * BLOCK + i + 1, :] = ls[j - 1]
            if i + j < BLOCK:
                for m in range(0, 4 - j):
                    band[m][i + j] = band[m][i + j] - ls[j - 1] * cs[j - 1 + m]
    solve(turned[4], factor, steps)
    moved = steps[...].T
    change = [moved[8 * q : 8 * q + 1, :] for q in range(3)]
    state[...] = jnp.concatenate(
        [coefs[q] + change[q] for q in range(3)] + [zero] + sums + [zero], axis=0
    )
    spline = Spline()
    field[LEAD : LEAD + ROWS, :] = spline.field(joined(change))
    dir_a, dir_b = directions(place_ref)
    slab_steps(pair_reader(meta_own, 1), 0, field, cross_early, (acc0, acc1))
    slab_steps(pair_reader(meta_own, dir_a), CAP, field, cross_early, (acc2, acc3))
    slab_steps(pair_reader(meta_own, dir_b), 0, field, cross_late, (acc4, acc5))
    part_out[0:1, :] = spline.adjoint(
        weight[...] * field[LEAD : LEAD + ROWS, :] - collected((acc0, acc1))
    )
    part_out[1:2, :] = -spline.adjoint(collected((acc2, acc3)))
    part_out[2:3, :] = -spline.adjoint(collected((acc4, acc5)))
    first = jnp.where(place_ref[4] == 0, 1.0, 0.0)
    half = iota((1, LANES), 1) < BLOCK
    part_out[3:4, :] = first * jnp.where(half, place_ref[1], place_ref[2]).astype(jnp.float32)
    part_out[4:8, :] = jnp.zeros((4, LANES), jnp.float32)


CHUNKS = 8


def final_kernel(
    place_ref, me, a, b, c, d, sb, sd, state, factor, grad_in, image_in,
    coef_out, warped_out,
    grad, image, field, steps, sems, out_sems,
):
    size = ROWS * 8 // CHUNKS
    at = [pl.ds(n * size, size) for n in range(CHUNKS)]
    loads = []
    for n in range(CHUNKS):
        loads.append(pltpu.make_async_copy(grad_in.at[at[n]], grad.at[at[n]], sems.at[0, n]))
        loads.append(pltpu.make_async_copy(image_in.at[at[n]], image.at[at[n]], sems.at[1, n]))
    for copy in loads:
        copy.start()
    steps[...] = jnp.zeros((LANES, LANES), jnp.float32)
    tiles = near_tiles(me, a, b, c, d, sb, sd)
    zero = jnp.zeros((1, LANES), jnp.float32)
    coefs = [state[q : q + 1, :] for q in range(3)]
    rows = []
    for q, block in enumerate(block_ids(place_ref)):
        gradsum = state[4 + q : 5 + q, :] + block_sums(tiles, block)
        rows += [-(gradsum + smooth_weight * pulled(coefs[q]))] + [zero] * 7
    solve(across(rows)[0:BLOCK, :], factor, steps)
    moved = steps[...].T
    coefs = [coefs[q] + moved[8 * q : 8 * q + 1, :] for q in range(3)]
    coef_out[...] = coefs[2][:, :BLOCK]
    spline = Spline()
    rigid = shift_step * place_ref[3].astype(jnp.float32)
    field[...] = spline.field(joined(coefs)) + rigid
    stores = []
    for n in range(CHUNKS):
        loads[2 * n].wait()
        loads[2 * n + 1].wait()

        def body(g, carry):
            for r in range(8):
                row = g * 8 + r
                rows = pl.ds(pl.multiple_of(row * 8, 8), 8)
                image[rows, :] = image[rows, :] + grad[rows, :] * field[pl.ds(row, 1), :]
            return carry

        lax.fori_loop(n * size // 64, (n + 1) * size // 64, body, 0)
        stores.append(pltpu.make_async_copy(image.at[at[n]], warped_out.at[at[n]], out_sems.at[n]))
        stores[-1].start()
    for copy in stores:
        copy.wait()


SMEM = pl.BlockSpec(memory_space=pltpu.SMEM)
VMEM = pl.BlockSpec(memory_space=pltpu.VMEM)
ANY = pl.BlockSpec(memory_space=pl.ANY)


def f32(*shape):
    return jax.ShapeDtypeStruct(shape, jnp.float32)


def call(kernel, name, in_specs, out_specs, out_shape, scratch):
    return pl.pallas_call(
        kernel,
        name=name,
        in_specs=in_specs,
        out_specs=out_specs,
        out_shape=out_shape,
        scratch_shapes=scratch,
        compiler_params=pltpu.CompilerParams(vmem_limit_bytes=VMEM_LIMIT),
    )


def whole():
    return pltpu.VMEM((PADDED * 8, LANES), jnp.float32)


def acc():
    return pltpu.VMEM((PADDED, LANES), jnp.float32)


def square():
    return pltpu.VMEM((LANES, LANES), jnp.float32)


def viewed(block):
    return block.reshape(DEPTH, ROWS, LANES).transpose(1, 0, 2).reshape(ROWS * DEPTH, LANES)


def per_device(images, gradient, shifts, tile_blocks, intersections, start_coefficients):
    tiles = lax.axis_size("tile")
    here = lax.axis_index("tile").astype(jnp.int32)
    knot = lax.axis_index("knot").astype(jnp.int32)
    ids = range(tiles)
    swap_a = [(i, i ^ 1) for i in ids]
    swap_b = [(i, ((i - 1) ^ 1) + 1) for i in ids if 0 < i < tiles - 1]
    swap_c = [(i, i + 3 if i % 2 else i - 3) for i in ids]
    swap_c = [(i, j) for i, j in swap_c if 0 <= j < tiles]
    same_d = [(i, i + 2 if i % 2 == 0 else i - 2) for i in ids]
    same_d = [(i, j) for i, j in same_d if 0 <= j < tiles]

    def move(value, route):
        return lax.ppermute(value, "tile", route)

    meta = intersections.reshape(-1)
    far_b = move(gradient, swap_b)
    far_a = move(gradient, swap_a)
    meta_a = move(meta, swap_a)
    meta_b = move(meta, swap_b)
    start = jnp.pad(start_coefficients, ((0, 7), (0, LANES - BLOCK)))
    slot = jnp.arange(4, dtype=jnp.int32)[:, None] == knot
    own = jnp.where(slot, start_coefficients, 0.0).reshape(2, LANES)
    own = lax.psum(jnp.pad(own, ((0, 6), (0, 0))), "knot")
    side_a = move(own, swap_a)
    side_b = move(own, swap_b)
    where = jnp.stack([here, tile_blocks[0, 0], tile_blocks[0, 1], shifts[0], knot])

    grad = viewed(gradient)
    image = viewed(images)
    cross_early, weight, field, part = call(
        early_kernel, "early_pairs",
        [SMEM] * 4 + [VMEM] * 3 + [ANY] * 3,
        [VMEM] * 4,
        [f32(2 * CAP, SLAB_ROWS, LANES), f32(ROWS, LANES), f32(PADDED, LANES), f32(8, LANES)],
        [whole()] * 3 + [acc()] * 5 + [pltpu.SemaphoreType.DMA((3,))],
    )(where, meta, meta_a, meta_b, own, side_a, side_b, grad, image, viewed(far_a))
    cross_late, part = call(
        late_kernel, "late_pairs",
        [SMEM] * 2 + [VMEM] * 2 + [ANY] * 3,
        [VMEM] * 2,
        [f32(CAP, SLAB_ROWS, LANES), f32(8, LANES)],
        [whole()] * 3 + [acc()] * 2 + [pltpu.SemaphoreType.DMA((3,))],
    )(where, meta, field, part, grad, image, viewed(far_b))

    def exchange(value):
        me = lax.psum(value, "knot")
        a = move(me, swap_a)
        b = move(me, swap_b)
        d = move(me, same_d)
        c = move(me, swap_c)
        sb = move(b, swap_a)
        sd = move(d, swap_a)
        return me, a, b, c, d, sb, sd

    part, state, factor = call(
        step_kernel, "first_step",
        [SMEM] * 2 + [VMEM] * 14,
        [VMEM] * 3,
        [f32(8, LANES), f32(8, LANES), f32(4 * BLOCK, LANES)],
        [acc(), square(), square()] + [acc()] * 6,
    )(where, meta, *exchange(part), own, side_a, side_b, start, weight, cross_early, cross_late)
    coef, warped = call(
        final_kernel, "second_step",
        [SMEM] + [VMEM] * 9 + [ANY] * 2,
        [VMEM, ANY],
        [f32(1, BLOCK), f32(ROWS * DEPTH, LANES)],
        [pltpu.VMEM((ROWS * DEPTH, LANES), jnp.float32)] * 2
        + [pltpu.VMEM((ROWS, LANES), jnp.float32), square()]
        + [pltpu.SemaphoreType.DMA((2, CHUNKS)), pltpu.SemaphoreType.DMA((CHUNKS,))],
    )(where, *exchange(part), state, factor, grad, image)
    warped = warped.reshape(ROWS, DEPTH, LANES).transpose(1, 0, 2).reshape(1, DEPTH, ROWS * LANES)
    return coef, warped


def solution(mesh):
    placed = (
        P("tile", "knot", None),
        P("tile", "knot", None),
        P("tile"),
        P("tile", None),
        P("tile", None, None, None),
        P(("tile", "knot"), None),
    )
    return jax.shard_map(
        per_device,
        mesh=mesh,
        in_specs=placed,
        out_specs=(P(("tile", "knot"), None), P("tile", "knot", None)),
        check_vma=False,
    )
```

```python
import functools

import jax
import jax.numpy as jnp
from jax import lax
from jax.experimental import pallas as pl
from jax.experimental.pallas import tpu as pltpu
from jax.sharding import PartitionSpec as P

SLAB = 8192
BLOCK = 64
LANES = 128
ROWS = 512
DEPTH = 8
LEAD = 16
PADDED = LEAD + ROWS + 16
GROUPS = SLAB // (8 * LANES) + 1
SLAB_ROWS = 8 * GROUPS
CAP = 8

shift_step = 0.05
smooth_weight = 20.0
ridge_weight = 1.0

EXACT = lax.Precision.HIGHEST
VMEM_LIMIT = 24 * 1024 * 1024


def iota(shape, dim):
    return lax.broadcasted_iota(jnp.int32, shape, dim)


def dot(a, b):
    return lax.dot_general(
        a, b, (((1,), (0,)), ((), ())), precision=EXACT, preferred_element_type=jnp.float32
    )


def dot_rows(a, b):
    return lax.dot_general(
        a, b, (((1,), (1,)), ((), ())), precision=EXACT, preferred_element_type=jnp.float32
    )


class Spline:
    def __init__(self):
        row = iota((ROWS, LANES), 0)
        lane = iota((ROWS, LANES), 1)
        self.low = (((row * LANES + lane) * 125) >> 16) == ((row * 125) >> 9)
        self.hot = (lane == ((row * 125) >> 9)).astype(jnp.float32)
        sub = iota((8, ROWS), 0)
        col = iota((8, ROWS), 1)
        first = (col * 125) >> 9
        centre = ((col * 256 + 127) * 125).astype(jnp.float32) * (1.0 / 131072.0)
        u = centre - first.astype(jnp.float32) - (sub >= 4).astype(jnp.float32)
        t = 1.0 - u
        k = 64.0 * 125.0 / 65536.0
        which = sub & 3
        def pick(a, b, c, d):
            return jnp.where(which == 0, a, jnp.where(which == 1, b, jnp.where(which == 2, c, d)))
        self.cubic = [
            pick(
                t * t * t / 6.0,
                2.0 / 3.0 - u * u + 0.5 * u * u * u,
                2.0 / 3.0 - t * t + 0.5 * t * t * t,
                u * u * u / 6.0,
            ),
            k * pick(-0.5 * t * t, -2.0 * u + 1.5 * u * u, 2.0 * t - 1.5 * t * t, 0.5 * u * u),
            (k * k) * pick(0.5 * t, 1.5 * u - 1.0, 1.5 * t - 1.0, 0.5 * u),
            (k * k * k) * pick(-1.0 / 6.0, 0.5, -0.5, 1.0 / 6.0),
        ]
        self.sub = sub
        eta = (iota((8, LANES), 1).astype(jnp.float32) - 63.5) * (1.0 / 64.0)
        power = iota((8, LANES), 0)
        q = jnp.ones((8, LANES), jnp.float32)
        for n in range(7):
            q = jnp.where(power > n, q * eta, q)
        self.powers = q

    def field(self, local):
        rows = [pltpu.roll(local, (LANES - s) % LANES, 1) if s else local for s in (0, 1, 2, 3)]
        rows += [pltpu.roll(local, LANES - s, 1) for s in (1, 2, 3, 4)]
        near = dot_rows(jnp.concatenate(rows, axis=0), self.hot)
        terms = jnp.concatenate([c * near for c in self.cubic], axis=0)
        wide = iota((32, 2 * LANES), 1)
        high = (iota((32, 2 * LANES), 0) & 4) != 0
        order = iota((32, 2 * LANES), 0) >> 3
        eta = ((wide & 127).astype(jnp.float32) - 63.5) * (1.0 / 64.0)
        power = jnp.where(
            order == 0, 1.0, jnp.where(order == 1, eta, jnp.where(order == 2, eta * eta, eta * eta * eta))
        )
        power = jnp.where(high == (wide >= LANES), power, 0.0)
        both = dot(terms.T, power)
        return jnp.where(self.low, both[:, :LANES], both[:, LANES:])

    def moments(self, value):
        low = jnp.where(self.low, value, 0.0)
        high = jnp.where(self.low, 0.0, value)
        a = dot_rows(self.powers, low)
        b = dot_rows(self.powers, high)
        return lambda n: jnp.where(self.sub < 4, a[n : n + 1], b[n : n + 1])

    def gather(self, rows):
        total = rows[0:1]
        for s in range(1, 4):
            total = total + pltpu.roll(rows[s : s + 1], s, 1)
        for s in range(4):
            total = total + pltpu.roll(rows[4 + s : 5 + s], s + 1, 1)
        return total

    def adjoint(self, value):
        part = self.moments(value)
        rows = sum(self.cubic[n] * part(n) for n in range(4))
        return self.gather(dot(rows, self.hot))

    def band(self, value):
        part = self.moments(value)
        parts = [part(n) for n in range(7)]
        y = [sum(self.cubic[j] * parts[i + j] for j in range(4)) for i in range(4)]
        stack = []
        for m in range(4):
            moved = [pltpu.roll(v, 8 - m, 0) if m else v for v in y]
            rows = sum(self.cubic[i] * moved[i] for i in range(4))
            stack.append(jnp.where((self.sub & 3) + m < 4, rows, 0.0))
        rows = dot(jnp.concatenate(stack, axis=0), self.hot)
        return [self.gather(rows[8 * m : 8 * m + 8]) for m in range(4)]


LAST_ROW = ROWS - SLAB_ROWS


class Here:
    def __init__(self, blocks=None, shifts=None):
        self.tile = lax.axis_index("tile").astype(jnp.int32)
        self.knot = lax.axis_index("knot").astype(jnp.int32)
        odd = self.tile & 1
        self.to_a = jnp.where(odd == 0, 2, 0)
        self.to_b = 2 - self.to_a
        if blocks is not None:
            self.blocks = [blocks[0, 0], blocks[0, 1]]
        if shifts is not None:
            self.rigid = shift_step * shifts[0].astype(jnp.float32)

    def block_row(self):
        lane = iota((1, LANES), 1)
        row = jnp.where(lane < BLOCK, self.blocks[0], self.blocks[1]).astype(jnp.float32)
        return jnp.where(self.knot == 0, 1.0, 0.0) * row

    def block_ids(self):
        owned = self.tile * 4 + self.knot
        return [b.astype(jnp.float32) for b in self.blocks + [owned]]


def place(pair, p):
    off_b, off_a = pair(p, 1), pair(p, 3)
    row_b = jnp.minimum(off_b >> 7, LAST_ROW)
    lead = off_b - row_b * LANES
    start = off_a - lead
    return row_b, lead, start >> 7, start & 127


def add_moved(accs, row_a, turn, i, value):
    lane = iota((8, LANES), 1)
    moved = pltpu.roll(value, turn, 1)
    keep = lane >= turn
    at = pl.ds(row_a + (LEAD + 8 * i), 8)
    accs[0][at, :] += jnp.where(keep, moved, 0.0)
    accs[1][at, :] += jnp.where(keep, 0.0, moved)


def live_count(pair):
    total = pair(0, 4)
    for p in range(1, CAP):
        total = total + pair(p, 4)
    return total


def pair_reader(ref, direction):
    return lambda p, field: ref[0, direction, p, field]


def slabs(pair, base, far, grad, image, cross, accs, field=None):
    lane = iota((8, LANES), 1)
    sub = iota((8, LANES), 0)

    def body(p, carry):
        row_b, lead, row_a, turn = place(pair, p)
        back = (LANES - turn) & 127
        keep = lane >= turn
        for i in range(GROUPS):
            c = jnp.zeros((8, LANES), jnp.float32)
            x = jnp.zeros((8, LANES), jnp.float32)
            for z in range(DEPTH):
                at_a = (row_a + (LEAD + 8 * i)) * 8 + z
                at_b = (row_b + 8 * i) * 8 + z
                at_g = at_b + LEAD * 8
                first = far[pl.ds(at_a, 8, stride=8), :]
                second = far[pl.ds(at_a + 8, 8, stride=8), :]
                slope = pltpu.roll(jnp.where(keep, first, second), back, 1)
                c = c + slope * grad[pl.ds(at_g, 8, stride=8), :]
                x = x + slope * image[pl.ds(at_b, 8, stride=8), :]
            if i in (0, 1, GROUPS - 1):
                s = (sub + 8 * i) * LANES + lane - lead
                valid = (s >= 0) & (s < SLAB)
                c = jnp.where(valid, c, 0.0)
                x = jnp.where(valid, x, 0.0)
            cross[base + p, 8 * i : 8 * i + 8, :] = c
            if field is not None:
                x = x + c * field[pl.ds(row_b + 8 * i, 8), :]
            add_moved(accs, row_a, turn, i, x)
        return carry

    lax.fori_loop(0, live_count(pair), body, 0)


def slab_steps(pair, base, field, cross, accs):
    def body(p, carry):
        row_b, lead, row_a, turn = place(pair, p)
        for i in range(GROUPS):
            c = cross[base + p, 8 * i : 8 * i + 8, :]
            value = c * field[pl.ds(row_b + 8 * i, 8), :]
            add_moved(accs, row_a, turn, i, value)
        return carry

    lax.fori_loop(0, live_count(pair), body, 0)


def collected(accs):
    return accs[0][LEAD : LEAD + ROWS, :] + accs[1][LEAD - 1 : LEAD + ROWS - 1, :]


def clear(refs):
    for ref in refs:
        ref[...] = jnp.zeros(ref.shape, jnp.float32)


def clear_ends(ref):
    ref[0 : LEAD * 8, :] = jnp.zeros((LEAD * 8, LANES), jnp.float32)
    ref[(LEAD + ROWS) * 8 :, :] = jnp.zeros(((PADDED - LEAD - ROWS) * 8, LANES), jnp.float32)


def local_values(here, own, side_a, side_b):
    out = []
    for block in here.blocks:
        col, slot = block >> 2, block & 3
        back = (here.knot - slot) & 3
        table = jnp.where(
            col == here.tile,
            own[...],
            jnp.where(col == (here.tile ^ 1), side_a[...], side_b[...]),
        )
        out.append(
            jnp.where(
                back == 0,
                table[0:1],
                jnp.where(back == 1, table[1:2], jnp.where(back == 2, table[2:3], table[3:4])),
            )
        )
    return jnp.concatenate(out, axis=1)


def padded_copy(source, target, sem):
    return pltpu.make_async_copy(source, target.at[pl.ds(LEAD * 8, ROWS * 8)], sem)


def cover(pair, count):
    lane = iota((8, LANES), 1)
    sub = iota((8, LANES), 0)

    def body(p, carry):
        off = pair(p, 3)
        for i in range(GROUPS):
            s = (sub + 8 * i) * LANES + lane - (off & 127)
            inside = (s >= 0) & (s < SLAB)
            count[pl.ds((off >> 7) + (LEAD + 8 * i), 8), :] += jnp.where(inside, 1.0, 0.0)
        return carry

    lax.fori_loop(0, live_count(pair), body, 0)


def early_kernel(
    meta, meta_a, grad_in, image_in, far_in,
    cross, weight_out, value_out, own_out, side_out, count, near, image,
    far, acc0, acc1, acc2, acc3, sems,
):
    copies = [
        padded_copy(grad_in, near, sems.at[0]),
        pltpu.make_async_copy(image_in, image, sems.at[1]),
        padded_copy(far_in, far, sems.at[2]),
    ]
    for c in copies:
        c.start()
    for ref in (near, far):
        clear_ends(ref)
    clear((acc0, acc1, acc2, acc3, count))
    here = Here()
    cover(pair_reader(meta, 1), count)
    cover(pair_reader(meta_a, 2 - here.to_a), count)

    def rows(g, carry):
        w = jnp.zeros((8, LANES), jnp.float32)
        v = jnp.zeros((8, LANES), jnp.float32)
        for z in range(DEPTH):
            slope = near[pl.ds(64 * g + (LEAD * 8 + z), 8, stride=8), :]
            w = w + slope * slope
            v = v + slope * image[pl.ds(64 * g + z, 8, stride=8), :]
        at = pl.ds(pl.multiple_of(8 * g, 8), 8)
        weight_out[at, :] = w
        value_out[at, :] = v
        return carry

    copies[0].wait()
    copies[1].wait()
    lax.fori_loop(0, ROWS // 8, rows, 0)
    slabs(pair_reader(meta, 1), 0, near, near, image, cross, (acc0, acc1))
    copies[2].wait()
    slabs(pair_reader(meta, here.to_a), CAP, far, near, image, cross, (acc2, acc3))
    own_out[...] = collected((acc0, acc1))
    side_out[...] = collected((acc2, acc3))


def late_kernel(
    meta, meta_b, blocks, shifts, column, side_a, side_b,
    near, image, cross_early, weight, value, own, side, counted, far_in,
    cross, weight_out, part_out,
    far, field, count, acc0, acc1, acc2, acc3, acc4, acc5, sems,
):
    copy = padded_copy(far_in, far, sems.at[0])
    copy.start()
    here = Here(blocks, shifts)
    clear_ends(far)
    clear((acc0, acc1, acc2, acc3, acc4, acc5))
    count[...] = counted[...]
    cover(pair_reader(meta_b, 2 - here.to_b), count)
    spline = Spline()
    field[...] = spline.field(local_values(here, column, side_a, side_b)) + here.rigid
    slab_steps(pair_reader(meta, 1), 0, field, cross_early, (acc0, acc1))
    slab_steps(pair_reader(meta, here.to_a), CAP, field, cross_early, (acc2, acc3))
    copy.wait()
    slabs(pair_reader(meta, here.to_b), 0, far, near, image, cross, (acc4, acc5), field)
    n = count[LEAD : LEAD + ROWS, :]
    w = weight[...] * n
    weight_out[...] = w
    part_out[0:1, :] = spline.adjoint(
        value[...] * n + w * field[...] - own[...] - collected((acc0, acc1))
    )
    part_out[1:2, :] = -spline.adjoint(side[...] + collected((acc2, acc3)))
    part_out[2:3, :] = -spline.adjoint(collected((acc4, acc5)))
    part_out[3:4, :] = here.block_row()
    for m, row in enumerate(spline.band(w)):
        part_out[4 + m : 5 + m, :] = row


def near_tiles(both, ahead, third, behind):
    me, a = both[0:8, :], both[8:16, :]
    d, b = ahead[0:8, :], ahead[8:16, :]
    sd, sb = behind[0:8, :], behind[8:16, :]
    c = third[...]
    return [
        (me, me[0:1] + a[1:2] + b[2:3]),
        (a, a[0:1] + me[1:2] + sb[2:3]),
        (b, b[0:1] + d[1:2] + me[2:3]),
        (d, d[0:1] + b[1:2] + c[2:3]),
        (sb, sb[0:1] + sd[1:2] + a[2:3]),
    ]


def folded(rows):
    return rows + pltpu.roll(rows, BLOCK, 1)


def block_sums(tiles, block):
    total = jnp.zeros((1, LANES), jnp.float32)
    for ref, grad in tiles:
        total = total + jnp.where(ref[3:4] == block, grad, 0.0)
    lane = iota((1, LANES), 1)
    return jnp.where(lane < BLOCK, folded(total), 0.0)


def pulled(coef):
    lane = iota((1, LANES), 1)
    y = coef - 2.0 * pltpu.roll(coef, LANES - 1, 1) + pltpu.roll(coef, LANES - 2, 1)
    y = jnp.where(lane < BLOCK - 2, y, 0.0)
    return jnp.where(lane < BLOCK, y - 2.0 * pltpu.roll(y, 1, 1) + pltpu.roll(y, 2, 1), 0.0)


def solve(target, factor, steps):
    y = []
    for i in range(BLOCK):
        v = target[i : i + 1, :]
        for j in range(1, 4):
            if i >= j:
                v = v - factor[j * BLOCK + i - j : j * BLOCK + i - j + 1, :] * y[i - j]
        y.append(v)
    x = [None] * BLOCK
    for i in reversed(range(BLOCK)):
        v = y[i] * factor[i : i + 1, :]
        for j in range(3, 0, -1):
            if i + j < BLOCK:
                v = v - factor[j * BLOCK + i : j * BLOCK + i + 1, :] * x[i + j]
        x[i] = v
        steps[i : i + 1, :] = v


def across(rows):
    block = jnp.concatenate(rows + [jnp.zeros((LANES - len(rows), LANES), jnp.float32)], axis=0)
    return block.T


def joined(coefs):
    lane = iota((1, LANES), 1)
    return jnp.where(lane < BLOCK, coefs[0], pltpu.roll(coefs[1], BLOCK, 1))


def step_kernel(
    meta, blocks, both, ahead, third, behind, column, side_a, side_b, start, weight,
    cross_early, cross_late,
    part_out, state, factor,
    field, steps, work, acc0, acc1, acc2, acc3, acc4, acc5,
):
    here = Here(blocks)
    clear((acc0, acc1, acc2, acc3, acc4, acc5, steps))
    lane = iota((1, LANES), 1)
    zero = jnp.zeros((1, LANES), jnp.float32)
    tiles = near_tiles(both, ahead, third, behind)
    knots = local_values(here, column, side_a, side_b)
    coefs = [
        jnp.where(lane < BLOCK, knots, 0.0),
        jnp.where(lane < BLOCK, pltpu.roll(knots, BLOCK, 1), 0.0),
        jnp.concatenate([start[...], jnp.zeros((1, LANES - BLOCK), jnp.float32)], axis=1),
    ]
    sums = []
    rows = []
    for q, block in enumerate(here.block_ids()):
        gradsum = block_sums(tiles, block)
        sums.append(gradsum)
        bands = []
        for m in range(4):
            total = zero
            for ref, _ in tiles:
                total = total + jnp.where(ref[3:4] == block, ref[4 + m : 5 + m], 0.0)
            total = jnp.where((lane & (BLOCK - 1)) + m < BLOCK, total, 0.0)
            bands.append(folded(total))
        inside = lambda cond: jnp.where(cond, 1.0, 0.0)
        upper, lower = inside(lane < BLOCK - 2), inside(lane >= 2)
        middle = inside((lane >= 1) & (lane < BLOCK - 1))
        bands[0] = bands[0] + smooth_weight * (upper + 4.0 * middle + lower) + ridge_weight
        bands[1] = bands[1] - smooth_weight * 2.0 * (
            upper + inside((lane >= 1) & (lane < BLOCK - 1))
        )
        bands[2] = bands[2] + smooth_weight * upper
        target = -(gradsum + smooth_weight * pulled(coefs[q]))
        rows += bands + [target, zero, zero, zero]
    work[...] = across(rows)
    turned = [work[0:BLOCK, :]] + [pltpu.roll(work[0:BLOCK, :], LANES - m, 1) for m in range(1, 5)]
    band = [[turned[m][i : i + 1, :] for i in range(BLOCK)] for m in range(4)]
    for i in range(BLOCK):
        r = 1.0 / band[0][i]
        factor[i : i + 1, :] = r
        cs = [band[m][i] for m in range(1, 4)]
        ls = [v * r for v in cs]
        for j in range(1, 4):
            factor[j * BLOCK + i : j * BLOCK + i + 1, :] = ls[j - 1]
            if i + j < BLOCK:
                for m in range(0, 4 - j):
                    band[m][i + j] = band[m][i + j] - ls[j - 1] * cs[j - 1 + m]
    solve(turned[4], factor, steps)
    moved = steps[...].T
    change = [moved[8 * q : 8 * q + 1, :] for q in range(3)]
    state[...] = jnp.concatenate(
        [coefs[q] + change[q] for q in range(3)] + [zero] + sums + [zero], axis=0
    )
    spline = Spline()
    field[...] = spline.field(joined(change))
    slab_steps(pair_reader(meta, 1), 0, field, cross_early, (acc0, acc1))
    slab_steps(pair_reader(meta, here.to_a), CAP, field, cross_early, (acc2, acc3))
    slab_steps(pair_reader(meta, here.to_b), 0, field, cross_late, (acc4, acc5))
    part_out[0:1, :] = spline.adjoint(weight[...] * field[...] - collected((acc0, acc1)))
    part_out[1:2, :] = -spline.adjoint(collected((acc2, acc3)))
    part_out[2:3, :] = -spline.adjoint(collected((acc4, acc5)))
    part_out[3:4, :] = here.block_row()
    part_out[4:8, :] = jnp.zeros((4, LANES), jnp.float32)


CHUNKS = 8


def final_kernel(
    blocks, shifts, both, ahead, third, behind, state, factor, grad_in, image_in,
    coef_out, warped_out,
    grad, image, field, steps, sems, out_sems,
):
    size = ROWS * 8 // CHUNKS
    at = [pl.ds(n * size, size) for n in range(CHUNKS)]
    loads = []
    for n in range(CHUNKS):
        loads.append(pltpu.make_async_copy(grad_in.at[at[n]], grad.at[at[n]], sems.at[0, n]))
        loads.append(pltpu.make_async_copy(image_in.at[at[n]], image.at[at[n]], sems.at[1, n]))
    for copy in loads:
        copy.start()
    here = Here(blocks, shifts)
    steps[...] = jnp.zeros((LANES, LANES), jnp.float32)
    tiles = near_tiles(both, ahead, third, behind)
    zero = jnp.zeros((1, LANES), jnp.float32)
    coefs = [state[q : q + 1, :] for q in range(3)]
    rows = []
    for q, block in enumerate(here.block_ids()):
        gradsum = state[4 + q : 5 + q, :] + block_sums(tiles, block)
        rows += [-(gradsum + smooth_weight * pulled(coefs[q]))] + [zero] * 7
    solve(across(rows)[0:BLOCK, :], factor, steps)
    moved = steps[...].T
    coefs = [coefs[q] + moved[8 * q : 8 * q + 1, :] for q in range(3)]
    coef_out[...] = coefs[2][:, :BLOCK]
    spline = Spline()
    field[...] = spline.field(joined(coefs)) + here.rigid
    stores = []
    for n in range(CHUNKS):
        loads[2 * n].wait()
        loads[2 * n + 1].wait()

        def body(g, carry):
            for r in range(8):
                row = g * 8 + r
                rows = pl.ds(pl.multiple_of(row * 8, 8), 8)
                image[rows, :] = image[rows, :] + grad[rows, :] * field[pl.ds(row, 1), :]
            return carry

        lax.fori_loop(n * size // 64, (n + 1) * size // 64, body, 0)
        stores.append(pltpu.make_async_copy(image.at[at[n]], warped_out.at[at[n]], out_sems.at[n]))
        stores[-1].start()
    for copy in stores:
        copy.wait()


SMEM = pl.BlockSpec(memory_space=pltpu.SMEM)
VMEM = pl.BlockSpec(memory_space=pltpu.VMEM)
ANY = pl.BlockSpec(memory_space=pl.ANY)


def f32(*shape):
    return jax.ShapeDtypeStruct(shape, jnp.float32)


def call(kernel, name, in_specs, out_specs, out_shape, scratch):
    return pl.pallas_call(
        kernel,
        name=name,
        in_specs=in_specs,
        out_specs=out_specs,
        out_shape=out_shape,
        scratch_shapes=scratch,
        compiler_params=pltpu.CompilerParams(vmem_limit_bytes=VMEM_LIMIT),
    )


def whole():
    return pltpu.VMEM((PADDED * 8, LANES), jnp.float32)


def acc():
    return pltpu.VMEM((PADDED, LANES), jnp.float32)


def square():
    return pltpu.VMEM((LANES, LANES), jnp.float32)


def viewed(block):
    return block.reshape(DEPTH, ROWS, LANES).transpose(1, 0, 2).reshape(ROWS * DEPTH, LANES)


def per_device(images, gradient, shifts, tile_blocks, intersections, start_coefficients):
    tiles = lax.axis_size("tile")
    knots = lax.axis_size("knot")
    ids = range(tiles)
    swap_a = [(i, i ^ 1) for i in ids]
    swap_b = [(i, ((i - 1) ^ 1) + 1) for i in ids if 0 < i < tiles - 1]
    swap_c = [(i, i + 3 if i % 2 else i - 3) for i in ids]
    swap_c = [(i, j) for i, j in swap_c if 0 <= j < tiles]
    same_d = [(i, i + 2 if i % 2 == 0 else i - 2) for i in ids]
    same_d = [(i, j) for i, j in same_d if 0 <= j < tiles]

    def move(value, route):
        return lax.ppermute(value, "tile", route)

    def over_knot(value):
        return [value] + [
            lax.ppermute(value, "knot", [(i, (i + s) % knots) for i in range(knots)])
            for s in range(1, knots)
        ]

    far_b = move(gradient, swap_b)
    far_a = move(gradient, swap_a)
    meta_a = move(intersections, swap_a)
    meta_b = move(intersections, swap_b)
    column = jnp.concatenate(over_knot(start_coefficients), axis=0)
    tables = (column, move(column, swap_a), move(column, swap_b))

    grad = viewed(gradient)
    image = viewed(images)
    cross_early, *sums, near, held = call(
        early_kernel, "early_pairs",
        [SMEM] * 2 + [ANY] * 3,
        [VMEM] * 8,
        [f32(2 * CAP, SLAB_ROWS, LANES)]
        + [f32(ROWS, LANES)] * 4
        + [f32(PADDED, LANES), f32(PADDED * DEPTH, LANES), f32(ROWS * DEPTH, LANES)],
        [whole()] + [acc()] * 4 + [pltpu.SemaphoreType.DMA((3,))],
    )(intersections, meta_a, grad, image, viewed(far_a))
    cross_late, weight, part = call(
        late_kernel, "late_pairs",
        [SMEM] * 4 + [VMEM] * 11 + [ANY],
        [VMEM] * 3,
        [f32(CAP, SLAB_ROWS, LANES), f32(ROWS, LANES), f32(8, LANES)],
        [whole(), pltpu.VMEM((ROWS, LANES), jnp.float32)]
        + [acc()] * 7
        + [pltpu.SemaphoreType.DMA((1,))],
    )(
        intersections, meta_b, tile_blocks, shifts, *tables, near, held, cross_early, *sums,
        viewed(far_b),
    )

    def exchange(value):
        v = over_knot(value)
        me = (v[0] + v[1]) + (v[2] + v[3])
        both = jnp.concatenate([me, move(me, swap_a)], axis=0)
        next_up = move(both, same_d)
        third = move(me, swap_c)
        next_up, third = lax.optimization_barrier((next_up, third))
        return both, next_up, third, move(next_up, swap_a)

    part, state, factor = call(
        step_kernel, "first_step",
        [SMEM] * 2 + [VMEM] * 11,
        [VMEM] * 3,
        [f32(8, LANES), f32(8, LANES), f32(4 * BLOCK, LANES)],
        [pltpu.VMEM((ROWS, LANES), jnp.float32), square(), square()] + [acc()] * 6,
    )(
        intersections, tile_blocks, *exchange(part), *tables, start_coefficients, weight,
        cross_early, cross_late,
    )
    coef, warped = call(
        final_kernel, "second_step",
        [SMEM] * 2 + [VMEM] * 6 + [ANY] * 2,
        [VMEM, ANY],
        [f32(1, BLOCK), f32(ROWS * DEPTH, LANES)],
        [pltpu.VMEM((ROWS * DEPTH, LANES), jnp.float32)] * 2
        + [pltpu.VMEM((ROWS, LANES), jnp.float32), square()]
        + [pltpu.SemaphoreType.DMA((2, CHUNKS)), pltpu.SemaphoreType.DMA((CHUNKS,))],
    )(tile_blocks, shifts, *exchange(part), state, factor, grad, image)
    warped = warped.reshape(ROWS, DEPTH, LANES).transpose(1, 0, 2).reshape(1, DEPTH, ROWS * LANES)
    return coef, warped


def solution(mesh):
    placed = (
        P("tile", "knot", None),
        P("tile", "knot", None),
        P("tile"),
        P("tile", None),
        P("tile", None, None, None),
        P(("tile", "knot"), None),
    )
    return jax.shard_map(
        per_device,
        mesh=mesh,
        in_specs=placed,
        out_specs=(P(("tile", "knot"), None), P("tile", "knot", None)),
        check_vma=False,
    )
```

```python
import functools

import jax
import jax.numpy as jnp
from jax import lax
from jax.experimental import pallas as pl
from jax.experimental.pallas import tpu as pltpu
from jax.sharding import PartitionSpec as P

SLAB = 8192
BLOCK = 64
LANES = 128
ROWS = 512
DEPTH = 8
LEAD = 16
PADDED = LEAD + ROWS + 16
GROUPS = SLAB // (8 * LANES) + 1
SLAB_ROWS = 8 * GROUPS
CAP = 8

shift_step = 0.05
smooth_weight = 20.0
ridge_weight = 1.0

EXACT = lax.Precision.HIGH


def iota(shape, dim):
    return lax.broadcasted_iota(jnp.int32, shape, dim)


def dot(a, b):
    return lax.dot_general(
        a, b, (((1,), (0,)), ((), ())), precision=EXACT, preferred_element_type=jnp.float32
    )


def dot_rows(a, b):
    return lax.dot_general(
        a, b, (((1,), (1,)), ((), ())), precision=EXACT, preferred_element_type=jnp.float32
    )


class Spline:
    def __init__(self):
        row = iota((ROWS, LANES), 0)
        lane = iota((ROWS, LANES), 1)
        self.low = (((row * LANES + lane) * 125) >> 16) == ((row * 125) >> 9)
        self.hot = (lane == ((row * 125) >> 9)).astype(jnp.float32)
        sub = iota((8, ROWS), 0)
        col = iota((8, ROWS), 1)
        first = (col * 125) >> 9
        centre = ((col * 256 + 127) * 125).astype(jnp.float32) * (1.0 / 131072.0)
        u = centre - first.astype(jnp.float32) - (sub >= 4).astype(jnp.float32)
        t = 1.0 - u
        k = 64.0 * 125.0 / 65536.0
        which = sub & 3
        def pick(a, b, c, d):
            return jnp.where(which == 0, a, jnp.where(which == 1, b, jnp.where(which == 2, c, d)))
        self.cubic = [
            pick(
                t * t * t / 6.0,
                2.0 / 3.0 - u * u + 0.5 * u * u * u,
                2.0 / 3.0 - t * t + 0.5 * t * t * t,
                u * u * u / 6.0,
            ),
            k * pick(-0.5 * t * t, -2.0 * u + 1.5 * u * u, 2.0 * t - 1.5 * t * t, 0.5 * u * u),
            (k * k) * pick(0.5 * t, 1.5 * u - 1.0, 1.5 * t - 1.0, 0.5 * u),
            (k * k * k) * pick(-1.0 / 6.0, 0.5, -0.5, 1.0 / 6.0),
        ]
        self.sub = sub
        eta = (iota((8, LANES), 1).astype(jnp.float32) - 63.5) * (1.0 / 64.0)
        power = iota((8, LANES), 0)
        q = jnp.ones((8, LANES), jnp.float32)
        for n in range(7):
            q = jnp.where(power > n, q * eta, q)
        self.powers = q

    def field(self, local):
        rows = [pltpu.roll(local, (LANES - s) % LANES, 1) if s else local for s in (0, 1, 2, 3)]
        rows += [pltpu.roll(local, LANES - s, 1) for s in (1, 2, 3, 4)]
        near = dot_rows(jnp.concatenate(rows, axis=0), self.hot)
        terms = jnp.concatenate([c * near for c in self.cubic], axis=0)
        wide = iota((32, 2 * LANES), 1)
        high = (iota((32, 2 * LANES), 0) & 4) != 0
        order = iota((32, 2 * LANES), 0) >> 3
        eta = ((wide & 127).astype(jnp.float32) - 63.5) * (1.0 / 64.0)
        power = jnp.where(
            order == 0, 1.0, jnp.where(order == 1, eta, jnp.where(order == 2, eta * eta, eta * eta * eta))
        )
        power = jnp.where(high == (wide >= LANES), power, 0.0)
        both = dot(terms.T, power)
        return jnp.where(self.low, both[:, :LANES], both[:, LANES:])

    def moments(self, value):
        low = jnp.where(self.low, value, 0.0)
        high = jnp.where(self.low, 0.0, value)
        a = dot_rows(self.powers, low)
        b = dot_rows(self.powers, high)
        return lambda n: jnp.where(self.sub < 4, a[n : n + 1], b[n : n + 1])

    def gather(self, rows):
        total = rows[0:1]
        for s in range(1, 4):
            total = total + pltpu.roll(rows[s : s + 1], s, 1)
        for s in range(4):
            total = total + pltpu.roll(rows[4 + s : 5 + s], s + 1, 1)
        return total

    def adjoint(self, value):
        part = self.moments(value)
        rows = sum(self.cubic[n] * part(n) for n in range(4))
        return self.gather(dot(rows, self.hot))

    def band(self, value):
        part = self.moments(value)
        parts = [part(n) for n in range(7)]
        y = [sum(self.cubic[j] * parts[i + j] for j in range(4)) for i in range(4)]
        stack = []
        for m in range(4):
            moved = [pltpu.roll(v, 8 - m, 0) if m else v for v in y]
            rows = sum(self.cubic[i] * moved[i] for i in range(4))
            stack.append(jnp.where((self.sub & 3) + m < 4, rows, 0.0))
        rows = dot(jnp.concatenate(stack, axis=0), self.hot)
        return [self.gather(rows[8 * m : 8 * m + 8]) for m in range(4)]


LAST_ROW = ROWS - SLAB_ROWS


class Here:
    def __init__(self, blocks=None, shifts=None):
        self.tile = lax.axis_index("tile").astype(jnp.int32)
        self.knot = lax.axis_index("knot").astype(jnp.int32)
        odd = self.tile & 1
        self.to_a = jnp.where(odd == 0, 2, 0)
        self.to_b = 2 - self.to_a
        self.side_b = self.tile + jnp.where(odd == 0, -1, 1)
        if blocks is not None:
            both = blocks[...].astype(jnp.float32)
            self.blocks = [jnp.broadcast_to(both[:, n : n + 1], (1, LANES)) for n in range(2)]
        if shifts is not None:
            self.rigid = shift_step * jnp.broadcast_to(
                shifts[...].astype(jnp.float32), (1, LANES)
            )

    def block_row(self):
        lane = iota((1, LANES), 1)
        row = jnp.where(lane < BLOCK, self.blocks[0], self.blocks[1])
        return jnp.where(self.knot == 0, 1.0, 0.0) * row

    def block_ids(self):
        owned = (self.tile * 4 + self.knot).astype(jnp.float32)
        return self.blocks + [jnp.full((1, LANES), owned)]


def place(pair, p):
    off_b, off_a = pair(p, 1), pair(p, 3)
    row_b = jnp.minimum(off_b >> 7, LAST_ROW)
    lead = off_b - row_b * LANES
    start = off_a - lead
    return row_b, lead, start >> 7, start & 127


def window(ref, row, rows=SLAB_ROWS):
    return ref.at[pl.ds(pl.multiple_of((row + LEAD) * 8, 8), rows * 8)]


def rows_at(row, plane):
    return pl.ds(row * 8 + plane, 8, stride=8)


def all_rows(plane, back=0):
    return pl.ds((LEAD - back) * 8 + plane, ROWS, stride=8)


def moved_sums(planes, plane, row_a, turn, values):
    keep = iota((8, LANES), 1) >= turn
    out = window(planes, row_a)
    sums = []
    for i, value in enumerate(values):
        moved = pltpu.roll(value, turn, 1)
        sums.append(
            (
                out[rows_at(8 * i, plane), :] + jnp.where(keep, moved, 0.0),
                out[rows_at(8 * i, plane + 1), :] + jnp.where(keep, 0.0, moved),
            )
        )

    def store():
        for i, (kept, passed) in enumerate(sums):
            out[rows_at(8 * i, plane), :] = kept
            out[rows_at(8 * i, plane + 1), :] = passed

    return store


def live_count(pair):
    total = pair(0, 4)
    for p in range(1, CAP):
        total = total + pair(p, 4)
    return total


def sent_reader(ref, direction):
    def read(p, field):
        at = (direction * CAP + p) * 5 + field
        return ref[4 + (at >> 6), at & 63].astype(jnp.int32)

    return read


FIELD, COUNT = 6, 7


def slabs(pair, base, far, grad, image, cross, planes, plane, with_field):
    lane = iota((8, LANES), 1)
    sub = iota((8, LANES), 0)

    def body(p, carry):
        row_b, lead, row_a, turn = place(pair, p)
        back = (LANES - turn) & 127
        keep = lane >= turn
        values = []
        far_rows = window(far, row_a, SLAB_ROWS + 8)
        grad_rows = window(grad, row_b)
        image_rows = window(image, row_b)
        field_rows = window(planes, row_b)
        for i in range(GROUPS):
            c = jnp.zeros((8, LANES), jnp.float32)
            x = jnp.zeros((8, LANES), jnp.float32)
            for z in range(DEPTH):
                first = far_rows[rows_at(8 * i, z), :]
                second = far_rows[rows_at(8 * i + 1, z), :]
                slope = pltpu.roll(jnp.where(keep, first, second), back, 1)
                c = c + slope * grad_rows[rows_at(8 * i, z), :]
                x = x + slope * image_rows[rows_at(8 * i, z), :]
            if i in (0, 1, GROUPS - 1):
                s = (sub + 8 * i) * LANES + lane - lead
                valid = (s >= 0) & (s < SLAB)
                c = jnp.where(valid, c, 0.0)
                x = jnp.where(valid, x, 0.0)
            cross[base + p, 8 * i : 8 * i + 8, :] = c
            if with_field:
                x = x + c * field_rows[rows_at(8 * i, FIELD), :]
            values.append(x)
        moved_sums(planes, plane, row_a, turn, values)()
        return carry

    lax.fori_loop(0, live_count(pair), body, 0)


def slab_steps(groups, planes):
    counts = [live_count(pair) for pair, _, _, _ in groups]
    total = functools.reduce(jnp.maximum, counts)

    def body(p, carry):
        done = []
        for (pair, base, cross, plane), count in zip(groups, counts):
            row_b, _, row_a, turn = place(pair, p)
            field_rows = window(planes, row_b)
            live = p < count
            values = [
                jnp.where(
                    live,
                    cross[base + p, 8 * i : 8 * i + 8, :] * field_rows[rows_at(8 * i, FIELD), :],
                    0.0,
                )
                for i in range(GROUPS)
            ]
            done.append(moved_sums(planes, plane, row_a, turn, values))
        for store in done:
            store()
        return carry

    lax.fori_loop(0, total, body, 0)


def collected(planes, plane):
    return planes[all_rows(plane), :] + planes[all_rows(plane + 1, 1), :]


def clear(refs):
    for ref in refs:
        ref[...] = jnp.zeros(ref.shape, jnp.float32)


def clear_ends(ref):
    ref[0 : LEAD * 8, :] = jnp.zeros((LEAD * 8, LANES), jnp.float32)
    ref[(LEAD + ROWS) * 8 :, :] = jnp.zeros(((PADDED - LEAD - ROWS) * 8, LANES), jnp.float32)


def local_values(here, tables):
    out = [jnp.zeros((1, BLOCK), jnp.float32) for _ in range(2)]
    for table, col in zip(tables, (here.tile, here.tile ^ 1, here.side_b)):
        for n in range(4):
            held = (col * 4 + ((here.knot - n) & 3)).astype(jnp.float32)
            for half in range(2):
                out[half] = jnp.where(
                    here.blocks[half][:, :BLOCK] == held, table[n : n + 1, :], out[half]
                )
    return jnp.concatenate(out, axis=1)


def scalar_copies(tables, scalars, sems):
    copies = [
        pltpu.make_async_copy(t, m, sems.at[n]) for n, (t, m) in enumerate(zip(tables, scalars))
    ]
    for c in copies:
        c.start()
    return copies


def padded_copy(source, target, sem):
    return pltpu.make_async_copy(source, target.at[pl.ds(LEAD * 8, ROWS * 8)], sem)


def cover(pair, planes):
    lane = iota((8, LANES), 1)
    sub = iota((8, LANES), 0)

    def body(p, carry):
        off = pair(p, 3)
        rows = window(planes, off >> 7)
        counts = [rows[rows_at(8 * i, COUNT), :] for i in range(GROUPS)]
        for i in range(GROUPS):
            s = (sub + 8 * i) * LANES + lane - (off & 127)
            inside = (s >= 0) & (s < SLAB)
            rows[rows_at(8 * i, COUNT), :] = counts[i] + jnp.where(inside, 1.0, 0.0)
        return carry

    lax.fori_loop(0, live_count(pair), body, 0)


def early_kernel(
    column, near, image, far_in,
    cross, weight_out, value_out, own_out, side_out, count_out,
    far, planes, scalars, sems,
):
    reads = scalar_copies((column,), (scalars,), sems)
    copy = padded_copy(far_in, far, sems.at[1])
    copy.start()
    clear_ends(far)
    clear((planes,))
    here = Here()

    def rows(g, carry):
        w = jnp.zeros((8, LANES), jnp.float32)
        v = jnp.zeros((8, LANES), jnp.float32)
        for z in range(DEPTH):
            slope = near[pl.ds(64 * g + (LEAD * 8 + z), 8, stride=8), :]
            w = w + slope * slope
            v = v + slope * image[pl.ds(64 * g + (LEAD * 8 + z), 8, stride=8), :]
        at = pl.ds(pl.multiple_of(8 * g, 8), 8)
        weight_out[at, :] = w
        value_out[at, :] = v
        return carry

    lax.fori_loop(0, ROWS // 8, rows, 0)
    reads[0].wait()
    cover(sent_reader(scalars, 1), planes)
    slabs(sent_reader(scalars, 1), 0, near, near, image, cross, planes, 0, False)
    copy.wait()
    slabs(sent_reader(scalars, here.to_a), CAP, far, near, image, cross, planes, 2, False)
    own_out[...] = collected(planes, 0)
    side_out[...] = collected(planes, 2)
    count_out[...] = planes[all_rows(COUNT), :]


def late_kernel(
    blocks, shifts, column, side_a, side_b,
    near, image, cross_early, weight, value, own, side, counted, far_in,
    cross, weight_out, part_out,
    far, planes, scalars_own, scalars_a, scalars_b, sems, scalar_sems,
):
    reads = scalar_copies(
        (column, side_a, side_b), (scalars_own, scalars_a, scalars_b), scalar_sems
    )
    copy = padded_copy(far_in, far, sems.at[0])
    copy.start()
    here = Here(blocks, shifts)
    clear_ends(far)
    clear((planes,))
    spline = Spline()
    field = spline.field(local_values(here, (column, side_a, side_b))) + here.rigid
    planes[all_rows(FIELD), :] = field
    for c in reads:
        c.wait()
    cover(sent_reader(scalars_a, 2 - here.to_a), planes)
    cover(sent_reader(scalars_b, 2 - here.to_b), planes)
    slab_steps(
        [
            (sent_reader(scalars_own, 1), 0, cross_early, 0),
            (sent_reader(scalars_own, here.to_a), CAP, cross_early, 2),
        ],
        planes,
    )
    copy.wait()
    slabs(sent_reader(scalars_own, here.to_b), 0, far, near, image, cross, planes, 4, True)
    n = counted[...] + planes[all_rows(COUNT), :]
    w = weight[...] * n
    weight_out[...] = w
    part_out[0:1, :] = spline.adjoint(
        value[...] * n + w * planes[all_rows(FIELD), :] - own[...] - collected(planes, 0)
    )
    part_out[1:2, :] = -spline.adjoint(side[...] + collected(planes, 2))
    part_out[2:3, :] = -spline.adjoint(collected(planes, 4))
    part_out[3:4, :] = here.block_row()
    for m, row in enumerate(spline.band(w)):
        part_out[4 + m : 5 + m, :] = row


def near_tiles(both, ahead, third, behind):
    me, a = both[0:8, :], both[8:16, :]
    d, b = ahead[0:8, :], ahead[8:16, :]
    sd, sb = behind[0:8, :], behind[8:16, :]
    c = third[...]
    return [
        (me, me[0:1] + a[1:2] + b[2:3]),
        (a, a[0:1] + me[1:2] + sb[2:3]),
        (b, b[0:1] + d[1:2] + me[2:3]),
        (d, d[0:1] + b[1:2] + c[2:3]),
        (sb, sb[0:1] + sd[1:2] + a[2:3]),
    ]


def folded(rows):
    return rows + pltpu.roll(rows, BLOCK, 1)


def block_sums(tiles, block):
    total = jnp.zeros((1, LANES), jnp.float32)
    for ref, grad in tiles:
        total = total + jnp.where(ref[3:4] == block, grad, 0.0)
    lane = iota((1, LANES), 1)
    return jnp.where(lane < BLOCK, folded(total), 0.0)


def pulled(coef):
    lane = iota((1, LANES), 1)
    y = coef - 2.0 * pltpu.roll(coef, LANES - 1, 1) + pltpu.roll(coef, LANES - 2, 1)
    y = jnp.where(lane < BLOCK - 2, y, 0.0)
    return jnp.where(lane < BLOCK, y - 2.0 * pltpu.roll(y, 1, 1) + pltpu.roll(y, 2, 1), 0.0)


def solve(target, factor, steps):
    y = []
    for i in range(BLOCK):
        v = target[i : i + 1, :]
        for j in range(1, 4):
            if i >= j:
                v = v - factor[j * BLOCK + i - j : j * BLOCK + i - j + 1, :] * y[i - j]
        y.append(v)
    x = [None] * BLOCK
    for i in reversed(range(BLOCK)):
        v = y[i] * factor[i : i + 1, :]
        for j in range(3, 0, -1):
            if i + j < BLOCK:
                v = v - factor[j * BLOCK + i : j * BLOCK + i + 1, :] * x[i + j]
        x[i] = v
        steps[i : i + 1, :] = v


def across(rows):
    block = jnp.concatenate(rows + [jnp.zeros((LANES - len(rows), LANES), jnp.float32)], axis=0)
    return block.T


def joined(coefs):
    lane = iota((1, LANES), 1)
    return jnp.where(lane < BLOCK, coefs[0], pltpu.roll(coefs[1], BLOCK, 1))


def step_kernel(
    blocks, both, ahead, third, behind, column, side_a, side_b, start, weight,
    cross_early, cross_late,
    part_out, state, factor,
    planes, steps, work, scalars, scalar_sems,
):
    reads = scalar_copies((column,), (scalars,), scalar_sems)
    here = Here(blocks)
    clear((planes, steps))
    lane = iota((1, LANES), 1)
    zero = jnp.zeros((1, LANES), jnp.float32)
    tiles = near_tiles(both, ahead, third, behind)
    knots = local_values(here, (column, side_a, side_b))
    coefs = [
        jnp.where(lane < BLOCK, knots, 0.0),
        jnp.where(lane < BLOCK, pltpu.roll(knots, BLOCK, 1), 0.0),
        jnp.concatenate([start[...], jnp.zeros((1, LANES - BLOCK), jnp.float32)], axis=1),
    ]
    sums = []
    rows = []
    for q, block in enumerate(here.block_ids()):
        gradsum = block_sums(tiles, block)
        sums.append(gradsum)
        bands = []
        for m in range(4):
            total = zero
            for ref, _ in tiles:
                total = total + jnp.where(ref[3:4] == block, ref[4 + m : 5 + m], 0.0)
            total = jnp.where((lane & (BLOCK - 1)) + m < BLOCK, total, 0.0)
            bands.append(folded(total))
        inside = lambda cond: jnp.where(cond, 1.0, 0.0)
        upper, lower = inside(lane < BLOCK - 2), inside(lane >= 2)
        middle = inside((lane >= 1) & (lane < BLOCK - 1))
        bands[0] = bands[0] + smooth_weight * (upper + 4.0 * middle + lower) + ridge_weight
        bands[1] = bands[1] - smooth_weight * 2.0 * (
            upper + inside((lane >= 1) & (lane < BLOCK - 1))
        )
        bands[2] = bands[2] + smooth_weight * upper
        target = -(gradsum + smooth_weight * pulled(coefs[q]))
        rows += bands + [target, zero, zero, zero]
    work[...] = across(rows)
    turned = [work[0:BLOCK, :]] + [pltpu.roll(work[0:BLOCK, :], LANES - m, 1) for m in range(1, 5)]
    band = [[turned[m][i : i + 1, :] for i in range(BLOCK)] for m in range(4)]
    for i in range(BLOCK):
        r = 1.0 / band[0][i]
        factor[i : i + 1, :] = r
        cs = [band[m][i] for m in range(1, 4)]
        ls = [v * r for v in cs]
        for j in range(1, 4):
            factor[j * BLOCK + i : j * BLOCK + i + 1, :] = ls[j - 1]
            if i + j < BLOCK:
                for m in range(0, 4 - j):
                    band[m][i + j] = band[m][i + j] - ls[j - 1] * cs[j - 1 + m]
    solve(turned[4], factor, steps)
    moved = steps[...].T
    change = [moved[8 * q : 8 * q + 1, :] for q in range(3)]
    state[...] = jnp.concatenate(
        [coefs[q] + change[q] for q in range(3)] + [zero] + sums + [zero], axis=0
    )
    spline = Spline()
    planes[all_rows(FIELD), :] = spline.field(joined(change))
    reads[0].wait()
    slab_steps(
        [
            (sent_reader(scalars, 1), 0, cross_early, 0),
            (sent_reader(scalars, here.to_a), CAP, cross_early, 2),
            (sent_reader(scalars, here.to_b), 0, cross_late, 4),
        ],
        planes,
    )
    part_out[0:1, :] = spline.adjoint(
        weight[...] * planes[all_rows(FIELD), :] - collected(planes, 0)
    )
    part_out[1:2, :] = -spline.adjoint(collected(planes, 2))
    part_out[2:3, :] = -spline.adjoint(collected(planes, 4))
    part_out[3:4, :] = here.block_row()
    part_out[4:8, :] = jnp.zeros((4, LANES), jnp.float32)


CHUNKS = 8


def final_kernel(
    blocks, shifts, both, ahead, third, behind, state, factor, grad_in, image_in,
    coef_out, warped_out,
    grad, image, field, steps, sems, out_sems,
):
    size = ROWS * 8 // CHUNKS
    at = [pl.ds(n * size, size) for n in range(CHUNKS)]
    loads = []
    for n in range(CHUNKS):
        loads.append(pltpu.make_async_copy(grad_in.at[at[n]], grad.at[at[n]], sems.at[0, n]))
        loads.append(pltpu.make_async_copy(image_in.at[at[n]], image.at[at[n]], sems.at[1, n]))
    for copy in loads:
        copy.start()
    here = Here(blocks, shifts)
    steps[...] = jnp.zeros((LANES, LANES), jnp.float32)
    tiles = near_tiles(both, ahead, third, behind)
    zero = jnp.zeros((1, LANES), jnp.float32)
    coefs = [state[q : q + 1, :] for q in range(3)]
    rows = []
    for q, block in enumerate(here.block_ids()):
        gradsum = state[4 + q : 5 + q, :] + block_sums(tiles, block)
        rows += [-(gradsum + smooth_weight * pulled(coefs[q]))] + [zero] * 7
    solve(across(rows)[0:BLOCK, :], factor, steps)
    moved = steps[...].T
    coefs = [coefs[q] + moved[8 * q : 8 * q + 1, :] for q in range(3)]
    coef_out[...] = coefs[2][:, :BLOCK]
    spline = Spline()
    field[...] = spline.field(joined(coefs)) + here.rigid
    stores = []
    for n in range(CHUNKS):
        loads[2 * n].wait()
        loads[2 * n + 1].wait()

        def body(g, carry):
            for r in range(8):
                row = g * 8 + r
                rows = pl.ds(pl.multiple_of(row * 8, 8), 8)
                image[rows, :] = image[rows, :] + grad[rows, :] * field[pl.ds(row, 1), :]
            return carry

        lax.fori_loop(n * size // 64, (n + 1) * size // 64, body, 0)
        stores.append(pltpu.make_async_copy(image.at[at[n]], warped_out.at[at[n]], out_sems.at[n]))
        stores[-1].start()
    for copy in stores:
        copy.wait()


VMEM = pl.BlockSpec(memory_space=pltpu.VMEM)
ANY = pl.BlockSpec(memory_space=pl.ANY)
HBM = pl.BlockSpec(memory_space=pltpu.HBM)


def f32(*shape):
    return jax.ShapeDtypeStruct(shape, jnp.float32)


def call(kernel, name, in_specs, out_specs, out_shape, scratch):
    return pl.pallas_call(
        kernel,
        name=name,
        in_specs=in_specs,
        out_specs=out_specs,
        out_shape=out_shape,
        scratch_shapes=scratch,
        compiler_params=pltpu.CompilerParams(vmem_limit_bytes=24 * 1024 * 1024),
    )


def whole():
    return pltpu.VMEM((PADDED * 8, LANES), jnp.float32)


def square():
    return pltpu.VMEM((LANES, LANES), jnp.float32)


def viewed(block):
    return block.reshape(DEPTH, ROWS, LANES).transpose(1, 0, 2).reshape(ROWS * DEPTH, LANES)


def per_device(images, gradient, shifts, tile_blocks, intersections, start_coefficients):
    tiles = lax.axis_size("tile")
    knots = lax.axis_size("knot")
    ids = range(tiles)
    swap_a = [(i, i ^ 1) for i in ids]
    swap_b = [(i, ((i - 1) ^ 1) + 1) for i in ids if 0 < i < tiles - 1]
    swap_c = [(i, i + 3 if i % 2 else i - 3) for i in ids]
    swap_c = [(i, j) for i, j in swap_c if 0 <= j < tiles]
    same_d = [(i, i + 2 if i % 2 == 0 else i - 2) for i in ids]
    same_d = [(i, j) for i, j in same_d if 0 <= j < tiles]

    def move(value, route):
        return lax.ppermute(value, "tile", route)

    def over_knot(value):
        return [value] + [
            lax.ppermute(value, "knot", [(i, (i + s) % knots) for i in range(knots)])
            for s in range(1, knots)
        ]

    shifts = shifts.reshape(1, 1)
    far_b = move(gradient, swap_b)
    far_a = move(gradient, swap_a)
    sent = jnp.pad(intersections.reshape(1, -1).astype(jnp.float32), ((0, 0), (0, 8)))
    column = jnp.concatenate(over_knot(start_coefficients) + [sent.reshape(2, BLOCK)], axis=0)
    side_a, side_b = move(column, swap_a), move(column, swap_b)

    grad, image = viewed(gradient), viewed(images)
    ends = ((LEAD * 8, (PADDED - LEAD - ROWS) * 8), (0, 0))
    near, held = jnp.pad(grad, ends), jnp.pad(image, ends)
    cross_early, *sums = call(
        early_kernel, "early_pairs",
        [VMEM] * 3 + [HBM],
        [VMEM] * 6,
        [f32(2 * CAP, SLAB_ROWS, LANES)] + [f32(ROWS, LANES)] * 5,
        [whole()] * 2 + [pltpu.SMEM((6, BLOCK), jnp.float32), pltpu.SemaphoreType.DMA((2,))],
    )(column, near, held, viewed(far_a))
    cross_late, weight, part = call(
        late_kernel, "late_pairs",
        [VMEM] * 13 + [ANY],
        [VMEM] * 3,
        [f32(CAP, SLAB_ROWS, LANES), f32(ROWS, LANES), f32(8, LANES)],
        [whole()] * 2
        + [pltpu.SMEM((6, BLOCK), jnp.float32)] * 3
        + [pltpu.SemaphoreType.DMA((1,)), pltpu.SemaphoreType.DMA((3,))],
    )(
        tile_blocks, shifts, column, side_a, side_b, near, held, cross_early, *sums,
        viewed(far_b),
    )

    def exchange(value):
        v = over_knot(value)
        me = (v[0] + v[1]) + (v[2] + v[3])
        third = move(me, swap_c)
        both = jnp.concatenate([me, move(me, swap_a)], axis=0)
        ahead = move(both, same_d)
        third, ahead = lax.optimization_barrier((third, ahead))
        return both, ahead, third, move(ahead, swap_a)

    part, state, factor = call(
        step_kernel, "first_step",
        [VMEM] * 12,
        [VMEM] * 3,
        [f32(8, LANES), f32(8, LANES), f32(4 * BLOCK, LANES)],
        [whole(), square(), square()]
        + [pltpu.SMEM((6, BLOCK), jnp.float32), pltpu.SemaphoreType.DMA((1,))],
    )(
        tile_blocks, *exchange(part), column, side_a, side_b, start_coefficients, weight,
        cross_early, cross_late,
    )
    coef, warped = call(
        final_kernel, "second_step",
        [VMEM] * 8 + [ANY] * 2,
        [VMEM, ANY],
        [f32(1, BLOCK), f32(ROWS * DEPTH, LANES)],
        [pltpu.VMEM((ROWS * DEPTH, LANES), jnp.float32)] * 2
        + [pltpu.VMEM((ROWS, LANES), jnp.float32), square()]
        + [pltpu.SemaphoreType.DMA((2, CHUNKS)), pltpu.SemaphoreType.DMA((CHUNKS,))],
    )(tile_blocks, shifts, *exchange(part), state, factor, grad, image)
    warped = warped.reshape(ROWS, DEPTH, LANES).transpose(1, 0, 2).reshape(1, DEPTH, ROWS * LANES)
    return coef, warped


def solution(mesh):
    placed = (
        P("tile", "knot", None),
        P("tile", "knot", None),
        P("tile"),
        P("tile", None),
        P("tile", None, None, None),
        P(("tile", "knot"), None),
    )
    return jax.shard_map(
        per_device,
        mesh=mesh,
        in_specs=placed,
        out_specs=(P(("tile", "knot"), None), P("tile", "knot", None)),
        check_vma=False,
    )
```

```python
import functools

import jax
import jax.numpy as jnp
from jax import lax
from jax.experimental import pallas as pl
from jax.experimental.pallas import tpu as pltpu
from jax.sharding import PartitionSpec as P

SLAB = 8192
BLOCK = 64
LANES = 128
ROWS = 512
DEPTH = 8
LEAD = 16
PADDED = LEAD + ROWS + 16
GROUPS = SLAB // (8 * LANES) + 1
SLAB_ROWS = 8 * GROUPS
CAP = 8

shift_step = 0.05
smooth_weight = 20.0
ridge_weight = 1.0

EXACT = lax.Precision.HIGH


def iota(shape, dim):
    return lax.broadcasted_iota(jnp.int32, shape, dim)


def dot(a, b):
    return lax.dot_general(
        a, b, (((1,), (0,)), ((), ())), precision=EXACT, preferred_element_type=jnp.float32
    )


def dot_rows(a, b):
    return lax.dot_general(
        a, b, (((1,), (1,)), ((), ())), precision=EXACT, preferred_element_type=jnp.float32
    )


class Spline:
    def __init__(self):
        row = iota((ROWS, LANES), 0)
        lane = iota((ROWS, LANES), 1)
        self.low = (((row * LANES + lane) * 125) >> 16) == ((row * 125) >> 9)
        self.hot = (lane == ((row * 125) >> 9)).astype(jnp.float32)
        sub = iota((8, ROWS), 0)
        col = iota((8, ROWS), 1)
        first = (col * 125) >> 9
        centre = ((col * 256 + 127) * 125).astype(jnp.float32) * (1.0 / 131072.0)
        u = centre - first.astype(jnp.float32) - (sub >= 4).astype(jnp.float32)
        t = 1.0 - u
        k = 64.0 * 125.0 / 65536.0
        which = sub & 3
        def pick(a, b, c, d):
            return jnp.where(which == 0, a, jnp.where(which == 1, b, jnp.where(which == 2, c, d)))
        self.cubic = [
            pick(
                t * t * t / 6.0,
                2.0 / 3.0 - u * u + 0.5 * u * u * u,
                2.0 / 3.0 - t * t + 0.5 * t * t * t,
                u * u * u / 6.0,
            ),
            k * pick(-0.5 * t * t, -2.0 * u + 1.5 * u * u, 2.0 * t - 1.5 * t * t, 0.5 * u * u),
            (k * k) * pick(0.5 * t, 1.5 * u - 1.0, 1.5 * t - 1.0, 0.5 * u),
            (k * k * k) * pick(-1.0 / 6.0, 0.5, -0.5, 1.0 / 6.0),
        ]
        self.sub = sub
        eta = (iota((8, LANES), 1).astype(jnp.float32) - 63.5) * (1.0 / 64.0)
        power = iota((8, LANES), 0)
        q = jnp.ones((8, LANES), jnp.float32)
        for n in range(7):
            q = jnp.where(power > n, q * eta, q)
        self.powers = q

    def field(self, local):
        rows = [pltpu.roll(local, (LANES - s) % LANES, 1) if s else local for s in (0, 1, 2, 3)]
        rows += [pltpu.roll(local, LANES - s, 1) for s in (1, 2, 3, 4)]
        near = dot_rows(jnp.concatenate(rows, axis=0), self.hot)
        terms = jnp.concatenate([c * near for c in self.cubic], axis=0)
        wide = iota((32, 2 * LANES), 1)
        high = (iota((32, 2 * LANES), 0) & 4) != 0
        order = iota((32, 2 * LANES), 0) >> 3
        eta = ((wide & 127).astype(jnp.float32) - 63.5) * (1.0 / 64.0)
        power = jnp.where(
            order == 0, 1.0, jnp.where(order == 1, eta, jnp.where(order == 2, eta * eta, eta * eta * eta))
        )
        power = jnp.where(high == (wide >= LANES), power, 0.0)
        both = dot(terms.T, power)
        return jnp.where(self.low, both[:, :LANES], both[:, LANES:])

    def moments(self, value):
        low = jnp.where(self.low, value, 0.0)
        high = jnp.where(self.low, 0.0, value)
        a = dot_rows(self.powers, low)
        b = dot_rows(self.powers, high)
        return lambda n: jnp.where(self.sub < 4, a[n : n + 1], b[n : n + 1])

    def gather(self, rows):
        total = rows[0:1]
        for s in range(1, 4):
            total = total + pltpu.roll(rows[s : s + 1], s, 1)
        for s in range(4):
            total = total + pltpu.roll(rows[4 + s : 5 + s], s + 1, 1)
        return total

    def adjoint(self, value):
        part = self.moments(value)
        rows = sum(self.cubic[n] * part(n) for n in range(4))
        return self.gather(dot(rows, self.hot))

    def band(self, value):
        part = self.moments(value)
        parts = [part(n) for n in range(7)]
        y = [sum(self.cubic[j] * parts[i + j] for j in range(4)) for i in range(4)]
        stack = []
        for m in range(4):
            moved = [pltpu.roll(v, 8 - m, 0) if m else v for v in y]
            rows = sum(self.cubic[i] * moved[i] for i in range(4))
            stack.append(jnp.where((self.sub & 3) + m < 4, rows, 0.0))
        rows = dot(jnp.concatenate(stack, axis=0), self.hot)
        return [self.gather(rows[8 * m : 8 * m + 8]) for m in range(4)]


LAST_ROW = ROWS - SLAB_ROWS


class Here:
    def __init__(self, blocks=None, shifts=None):
        self.tile = lax.axis_index("tile").astype(jnp.int32)
        self.knot = lax.axis_index("knot").astype(jnp.int32)
        odd = self.tile & 1
        self.to_a = jnp.where(odd == 0, 2, 0)
        self.to_b = 2 - self.to_a
        self.side_b = self.tile + jnp.where(odd == 0, -1, 1)
        if blocks is not None:
            both = blocks[...].astype(jnp.float32)
            self.blocks = [jnp.broadcast_to(both[:, n : n + 1], (1, LANES)) for n in range(2)]
        if shifts is not None:
            self.rigid = shift_step * jnp.broadcast_to(
                shifts[...].astype(jnp.float32), (1, LANES)
            )

    def block_row(self):
        lane = iota((1, LANES), 1)
        row = jnp.where(lane < BLOCK, self.blocks[0], self.blocks[1])
        return jnp.where(self.knot == 0, 1.0, 0.0) * row

    def block_ids(self):
        owned = (self.tile * 4 + self.knot).astype(jnp.float32)
        return self.blocks + [jnp.full((1, LANES), owned)]


def place(pair, p):
    off_b, off_a = pair(p, 1), pair(p, 3)
    row_b = jnp.minimum(off_b >> 7, LAST_ROW)
    lead = off_b - row_b * LANES
    start = off_a - lead
    return row_b, lead, start >> 7, start & 127


def window(ref, row, rows=SLAB_ROWS):
    return ref.at[pl.ds(pl.multiple_of((row + LEAD) * 8, 8), rows * 8)]


def rows_at(row, plane):
    return pl.ds(row * 8 + plane, 8, stride=8)


def all_rows(plane, back=0):
    return pl.ds((LEAD - back) * 8 + plane, ROWS, stride=8)


def moved_sums(planes, plane, row_a, turn, values):
    keep = iota((8, LANES), 1) >= turn
    out = window(planes, row_a)
    sums = []
    for i, value in enumerate(values):
        moved = pltpu.roll(value, turn, 1)
        sums.append(
            (
                out[rows_at(8 * i, plane), :] + jnp.where(keep, moved, 0.0),
                out[rows_at(8 * i, plane + 1), :] + jnp.where(keep, 0.0, moved),
            )
        )

    def store():
        for i, (kept, passed) in enumerate(sums):
            out[rows_at(8 * i, plane), :] = kept
            out[rows_at(8 * i, plane + 1), :] = passed

    return store


def live_count(pair):
    total = pair(0, 4)
    for p in range(1, CAP):
        total = total + pair(p, 4)
    return total


def sent_reader(ref, direction):
    def read(p, field):
        at = (direction * CAP + p) * 5 + field
        return ref[4 + (at >> 6), at & 63].astype(jnp.int32)

    return read


FIELD, COUNT = 6, 7


def slabs(pair, base, far, grad, image, cross, planes, plane, with_field):
    lane = iota((8, LANES), 1)
    sub = iota((8, LANES), 0)

    def body(p, carry):
        row_b, lead, row_a, turn = place(pair, p)
        back = (LANES - turn) & 127
        keep = lane >= turn
        values = []
        far_rows = window(far, row_a, SLAB_ROWS + 8)
        grad_rows = window(grad, row_b)
        image_rows = window(image, row_b)
        field_rows = window(planes, row_b)
        for i in range(GROUPS):
            c = jnp.zeros((8, LANES), jnp.float32)
            x = jnp.zeros((8, LANES), jnp.float32)
            for z in range(DEPTH):
                first = far_rows[rows_at(8 * i, z), :]
                second = far_rows[rows_at(8 * i + 1, z), :]
                slope = pltpu.roll(jnp.where(keep, first, second), back, 1)
                c = c + slope * grad_rows[rows_at(8 * i, z), :]
                x = x + slope * image_rows[rows_at(8 * i, z), :]
            if i in (0, 1, GROUPS - 1):
                s = (sub + 8 * i) * LANES + lane - lead
                valid = (s >= 0) & (s < SLAB)
                c = jnp.where(valid, c, 0.0)
                x = jnp.where(valid, x, 0.0)
            cross[base + p, 8 * i : 8 * i + 8, :] = c
            if with_field:
                x = x + c * field_rows[rows_at(8 * i, FIELD), :]
            values.append(x)
        moved_sums(planes, plane, row_a, turn, values)()
        return carry

    lax.fori_loop(0, live_count(pair), body, 0)


def slab_steps(groups, planes):
    counts = [live_count(pair) for pair, _, _, _ in groups]
    total = functools.reduce(jnp.maximum, counts)

    def body(p, carry):
        done = []
        for (pair, base, cross, plane), count in zip(groups, counts):
            row_b, _, row_a, turn = place(pair, p)
            field_rows = window(planes, row_b)
            live = p < count
            values = [
                jnp.where(
                    live,
                    cross[base + p, 8 * i : 8 * i + 8, :] * field_rows[rows_at(8 * i, FIELD), :],
                    0.0,
                )
                for i in range(GROUPS)
            ]
            done.append(moved_sums(planes, plane, row_a, turn, values))
        for store in done:
            store()
        return carry

    lax.fori_loop(0, total, body, 0)


def collected(planes, plane):
    return planes[all_rows(plane), :] + planes[all_rows(plane + 1, 1), :]


def clear(refs):
    for ref in refs:
        ref[...] = jnp.zeros(ref.shape, jnp.float32)


def clear_ends(ref):
    ref[0 : LEAD * 8, :] = jnp.zeros((LEAD * 8, LANES), jnp.float32)
    ref[(LEAD + ROWS) * 8 :, :] = jnp.zeros(((PADDED - LEAD - ROWS) * 8, LANES), jnp.float32)


def local_values(here, tables):
    out = [jnp.zeros((1, BLOCK), jnp.float32) for _ in range(2)]
    for table, col in zip(tables, (here.tile, here.tile ^ 1, here.side_b)):
        for n in range(4):
            held = (col * 4 + ((here.knot - n) & 3)).astype(jnp.float32)
            for half in range(2):
                out[half] = jnp.where(
                    here.blocks[half][:, :BLOCK] == held, table[n : n + 1, :], out[half]
                )
    return jnp.concatenate(out, axis=1)


def scalar_copies(tables, scalars, sems):
    copies = [
        pltpu.make_async_copy(t, m, sems.at[n]) for n, (t, m) in enumerate(zip(tables, scalars))
    ]
    for c in copies:
        c.start()
    return copies


def padded_copy(source, target, sem):
    return pltpu.make_async_copy(source, target.at[pl.ds(LEAD * 8, ROWS * 8)], sem)


def cover(pair, planes):
    lane = iota((8, LANES), 1)
    sub = iota((8, LANES), 0)

    def body(p, carry):
        off = pair(p, 3)
        rows = window(planes, off >> 7)
        counts = [rows[rows_at(8 * i, COUNT), :] for i in range(GROUPS)]
        for i in range(GROUPS):
            s = (sub + 8 * i) * LANES + lane - (off & 127)
            inside = (s >= 0) & (s < SLAB)
            rows[rows_at(8 * i, COUNT), :] = counts[i] + jnp.where(inside, 1.0, 0.0)
        return carry

    lax.fori_loop(0, live_count(pair), body, 0)


def early_kernel(
    column, near, image, far_in,
    cross, weight_out, value_out, own_out, side_out, count_out,
    far, planes, scalars, sems,
):
    reads = scalar_copies((column,), (scalars,), sems)
    copy = padded_copy(far_in, far, sems.at[1])
    copy.start()
    clear_ends(far)
    clear((planes,))
    here = Here()

    def rows(g, carry):
        w = jnp.zeros((8, LANES), jnp.float32)
        v = jnp.zeros((8, LANES), jnp.float32)
        for z in range(DEPTH):
            slope = near[pl.ds(64 * g + (LEAD * 8 + z), 8, stride=8), :]
            w = w + slope * slope
            v = v + slope * image[pl.ds(64 * g + (LEAD * 8 + z), 8, stride=8), :]
        at = pl.ds(pl.multiple_of(8 * g, 8), 8)
        weight_out[at, :] = w
        value_out[at, :] = v
        return carry

    lax.fori_loop(0, ROWS // 8, rows, 0)
    reads[0].wait()
    cover(sent_reader(scalars, 1), planes)
    slabs(sent_reader(scalars, 1), 0, near, near, image, cross, planes, 0, False)
    copy.wait()
    slabs(sent_reader(scalars, here.to_a), CAP, far, near, image, cross, planes, 2, False)
    own_out[...] = collected(planes, 0)
    side_out[...] = collected(planes, 2)
    count_out[...] = planes[all_rows(COUNT), :]


def late_kernel(
    blocks, shifts, column, side_a, side_b,
    near, image, cross_early, weight, value, own, side, counted, far_in,
    cross, weight_out, part_out,
    far, planes, scalars_own, scalars_a, scalars_b, sems, scalar_sems,
):
    reads = scalar_copies(
        (column, side_a, side_b), (scalars_own, scalars_a, scalars_b), scalar_sems
    )
    copy = padded_copy(far_in, far, sems.at[0])
    copy.start()
    here = Here(blocks, shifts)
    clear_ends(far)
    clear((planes,))
    spline = Spline()
    field = spline.field(local_values(here, (column, side_a, side_b))) + here.rigid
    planes[all_rows(FIELD), :] = field
    for c in reads:
        c.wait()
    cover(sent_reader(scalars_a, 2 - here.to_a), planes)
    cover(sent_reader(scalars_b, 2 - here.to_b), planes)
    slab_steps(
        [
            (sent_reader(scalars_own, 1), 0, cross_early, 0),
            (sent_reader(scalars_own, here.to_a), CAP, cross_early, 2),
        ],
        planes,
    )
    copy.wait()
    slabs(sent_reader(scalars_own, here.to_b), 0, far, near, image, cross, planes, 4, True)
    n = counted[...] + planes[all_rows(COUNT), :]
    w = weight[...] * n
    weight_out[...] = w
    part_out[0:1, :] = spline.adjoint(
        value[...] * n + w * planes[all_rows(FIELD), :] - own[...] - collected(planes, 0)
    )
    part_out[1:2, :] = -spline.adjoint(side[...] + collected(planes, 2))
    part_out[2:3, :] = -spline.adjoint(collected(planes, 4))
    part_out[3:4, :] = here.block_row()
    for m, row in enumerate(spline.band(w)):
        part_out[4 + m : 5 + m, :] = row


def near_tiles(both, ahead, third, behind):
    me, a = both[0:8, :], both[8:16, :]
    d, b = ahead[0:8, :], ahead[8:16, :]
    sd, sb = behind[0:8, :], behind[8:16, :]
    c = third[0:8, :]
    return [
        (me, me[0:1] + a[1:2] + b[2:3]),
        (a, a[0:1] + me[1:2] + sb[2:3]),
        (b, b[0:1] + d[1:2] + me[2:3]),
        (d, d[0:1] + b[1:2] + c[2:3]),
        (sb, sb[0:1] + sd[1:2] + a[2:3]),
    ]


def folded(rows):
    return rows + pltpu.roll(rows, BLOCK, 1)


def block_sums(tiles, block):
    total = jnp.zeros((1, LANES), jnp.float32)
    for ref, grad in tiles:
        total = total + jnp.where(ref[3:4] == block, grad, 0.0)
    lane = iota((1, LANES), 1)
    return jnp.where(lane < BLOCK, folded(total), 0.0)


def pulled(coef):
    lane = iota((1, LANES), 1)
    y = coef - 2.0 * pltpu.roll(coef, LANES - 1, 1) + pltpu.roll(coef, LANES - 2, 1)
    y = jnp.where(lane < BLOCK - 2, y, 0.0)
    return jnp.where(lane < BLOCK, y - 2.0 * pltpu.roll(y, 1, 1) + pltpu.roll(y, 2, 1), 0.0)


def solve(target, factor, steps):
    y = []
    for i in range(BLOCK):
        v = target[i : i + 1, :]
        for j in range(1, 4):
            if i >= j:
                v = v - factor[j * BLOCK + i - j : j * BLOCK + i - j + 1, :] * y[i - j]
        y.append(v)
    x = [None] * BLOCK
    for i in reversed(range(BLOCK)):
        v = y[i] * factor[i : i + 1, :]
        for j in range(3, 0, -1):
            if i + j < BLOCK:
                v = v - factor[j * BLOCK + i : j * BLOCK + i + 1, :] * x[i + j]
        x[i] = v
        steps[i : i + 1, :] = v


def across(rows):
    block = jnp.concatenate(rows + [jnp.zeros((LANES - len(rows), LANES), jnp.float32)], axis=0)
    return block.T


def joined(coefs):
    lane = iota((1, LANES), 1)
    return jnp.where(lane < BLOCK, coefs[0], pltpu.roll(coefs[1], BLOCK, 1))


def step_kernel(
    blocks, both, ahead, third, behind, column, side_a, side_b, start, weight,
    cross_early, cross_late,
    part_out, state, factor,
    planes, steps, work, scalars, scalar_sems,
):
    reads = scalar_copies((column,), (scalars,), scalar_sems)
    here = Here(blocks)
    clear((planes, steps))
    lane = iota((1, LANES), 1)
    zero = jnp.zeros((1, LANES), jnp.float32)
    tiles = near_tiles(both, ahead, third, behind)
    knots = local_values(here, (column, side_a, side_b))
    coefs = [
        jnp.where(lane < BLOCK, knots, 0.0),
        jnp.where(lane < BLOCK, pltpu.roll(knots, BLOCK, 1), 0.0),
        jnp.concatenate([start[...], jnp.zeros((1, LANES - BLOCK), jnp.float32)], axis=1),
    ]
    sums = []
    rows = []
    for q, block in enumerate(here.block_ids()):
        gradsum = block_sums(tiles, block)
        sums.append(gradsum)
        bands = []
        for m in range(4):
            total = zero
            for ref, _ in tiles:
                total = total + jnp.where(ref[3:4] == block, ref[4 + m : 5 + m], 0.0)
            total = jnp.where((lane & (BLOCK - 1)) + m < BLOCK, total, 0.0)
            bands.append(folded(total))
        inside = lambda cond: jnp.where(cond, 1.0, 0.0)
        upper, lower = inside(lane < BLOCK - 2), inside(lane >= 2)
        middle = inside((lane >= 1) & (lane < BLOCK - 1))
        bands[0] = bands[0] + smooth_weight * (upper + 4.0 * middle + lower) + ridge_weight
        bands[1] = bands[1] - smooth_weight * 2.0 * (
            upper + inside((lane >= 1) & (lane < BLOCK - 1))
        )
        bands[2] = bands[2] + smooth_weight * upper
        target = -(gradsum + smooth_weight * pulled(coefs[q]))
        rows += bands + [target, zero, zero, zero]
    work[...] = across(rows)
    turned = [work[0:BLOCK, :]] + [pltpu.roll(work[0:BLOCK, :], LANES - m, 1) for m in range(1, 5)]
    band = [[turned[m][i : i + 1, :] for i in range(BLOCK)] for m in range(4)]
    for i in range(BLOCK):
        r = 1.0 / band[0][i]
        factor[i : i + 1, :] = r
        cs = [band[m][i] for m in range(1, 4)]
        ls = [v * r for v in cs]
        for j in range(1, 4):
            factor[j * BLOCK + i : j * BLOCK + i + 1, :] = ls[j - 1]
            if i + j < BLOCK:
                for m in range(0, 4 - j):
                    band[m][i + j] = band[m][i + j] - ls[j - 1] * cs[j - 1 + m]
    solve(turned[4], factor, steps)
    moved = steps[...].T
    change = [moved[8 * q : 8 * q + 1, :] for q in range(3)]
    state[...] = jnp.concatenate(
        [coefs[q] + change[q] for q in range(3)] + [zero] + sums + [zero], axis=0
    )
    spline = Spline()
    planes[all_rows(FIELD), :] = spline.field(joined(change))
    reads[0].wait()
    slab_steps(
        [
            (sent_reader(scalars, 1), 0, cross_early, 0),
            (sent_reader(scalars, here.to_a), CAP, cross_early, 2),
            (sent_reader(scalars, here.to_b), 0, cross_late, 4),
        ],
        planes,
    )
    part_out[0:1, :] = spline.adjoint(
        weight[...] * planes[all_rows(FIELD), :] - collected(planes, 0)
    )
    part_out[1:2, :] = -spline.adjoint(collected(planes, 2))
    part_out[2:3, :] = -spline.adjoint(collected(planes, 4))
    part_out[3:4, :] = here.block_row()
    part_out[4:8, :] = jnp.zeros((4, LANES), jnp.float32)


CHUNKS = 8


def final_kernel(
    blocks, shifts, both, ahead, third, behind, state, factor, grad_in, image_in,
    coef_out, warped_out,
    grad, image, field, steps, sems, out_sems,
):
    size = ROWS * 8 // CHUNKS
    at = [pl.ds(n * size, size) for n in range(CHUNKS)]
    loads = []
    for n in range(CHUNKS):
        loads.append(pltpu.make_async_copy(grad_in.at[at[n]], grad.at[at[n]], sems.at[0, n]))
        loads.append(pltpu.make_async_copy(image_in.at[at[n]], image.at[at[n]], sems.at[1, n]))
    for copy in loads:
        copy.start()
    here = Here(blocks, shifts)
    steps[...] = jnp.zeros((LANES, LANES), jnp.float32)
    tiles = near_tiles(both, ahead, third, behind)
    zero = jnp.zeros((1, LANES), jnp.float32)
    coefs = [state[q : q + 1, :] for q in range(3)]
    rows = []
    for q, block in enumerate(here.block_ids()):
        gradsum = state[4 + q : 5 + q, :] + block_sums(tiles, block)
        rows += [-(gradsum + smooth_weight * pulled(coefs[q]))] + [zero] * 7
    solve(across(rows)[0:BLOCK, :], factor, steps)
    moved = steps[...].T
    coefs = [coefs[q] + moved[8 * q : 8 * q + 1, :] for q in range(3)]
    coef_out[...] = coefs[2][:, :BLOCK]
    spline = Spline()
    field[...] = spline.field(joined(coefs)) + here.rigid
    stores = []
    for n in range(CHUNKS):
        loads[2 * n].wait()
        loads[2 * n + 1].wait()

        def body(g, carry):
            for r in range(8):
                row = g * 8 + r
                rows = pl.ds(pl.multiple_of(row * 8, 8), 8)
                image[rows, :] = image[rows, :] + grad[rows, :] * field[pl.ds(row, 1), :]
            return carry

        lax.fori_loop(n * size // 64, (n + 1) * size // 64, body, 0)
        stores.append(pltpu.make_async_copy(image.at[at[n]], warped_out.at[at[n]], out_sems.at[n]))
        stores[-1].start()
    for copy in stores:
        copy.wait()


VMEM = pl.BlockSpec(memory_space=pltpu.VMEM)
ANY = pl.BlockSpec(memory_space=pl.ANY)
HBM = pl.BlockSpec(memory_space=pltpu.HBM)


def f32(*shape):
    return jax.ShapeDtypeStruct(shape, jnp.float32)


def call(kernel, name, in_specs, out_specs, out_shape, scratch):
    return pl.pallas_call(
        kernel,
        name=name,
        in_specs=in_specs,
        out_specs=out_specs,
        out_shape=out_shape,
        scratch_shapes=scratch,
        compiler_params=pltpu.CompilerParams(vmem_limit_bytes=24 * 1024 * 1024),
    )


def whole():
    return pltpu.VMEM((PADDED * 8, LANES), jnp.float32)


def square():
    return pltpu.VMEM((LANES, LANES), jnp.float32)


def viewed(block):
    return block.reshape(DEPTH, ROWS, LANES).transpose(1, 0, 2).reshape(ROWS * DEPTH, LANES)


def per_device(images, gradient, shifts, tile_blocks, intersections, start_coefficients):
    tiles = lax.axis_size("tile")
    knots = lax.axis_size("knot")
    ids = range(tiles)
    swap_a = [(i, i ^ 1) for i in ids]
    swap_b = [(i, ((i - 1) ^ 1) + 1) for i in ids if 0 < i < tiles - 1]
    swap_c = [(i, i + 3 if i % 2 else i - 3) for i in ids]
    swap_c = [(i, j) for i, j in swap_c if 0 <= j < tiles]
    same_d = [(i, i + 2 if i % 2 == 0 else i - 2) for i in ids]
    same_d = [(i, j) for i, j in same_d if 0 <= j < tiles]

    def move(value, route):
        return lax.ppermute(value, "tile", route)

    def over_knot(value):
        return [value] + [
            lax.ppermute(value, "knot", [(i, (i + s) % knots) for i in range(knots)])
            for s in range(1, knots)
        ]

    shifts = shifts.reshape(1, 1)
    far_b = move(gradient, swap_b)
    far_a = move(gradient, swap_a)
    sent = jnp.pad(intersections.reshape(1, -1).astype(jnp.float32), ((0, 0), (0, 8)))
    column = jnp.concatenate(over_knot(start_coefficients) + [sent.reshape(2, BLOCK)], axis=0)
    side_a, side_b = move(column, swap_a), move(column, swap_b)

    grad, image = viewed(gradient), viewed(images)
    ends = ((LEAD * 8, (PADDED - LEAD - ROWS) * 8), (0, 0))
    near, held = jnp.pad(grad, ends), jnp.pad(image, ends)
    cross_early, *sums = call(
        early_kernel, "early_pairs",
        [VMEM] * 3 + [HBM],
        [VMEM] * 6,
        [f32(2 * CAP, SLAB_ROWS, LANES)] + [f32(ROWS, LANES)] * 5,
        [whole()] * 2 + [pltpu.SMEM((6, BLOCK), jnp.float32), pltpu.SemaphoreType.DMA((2,))],
    )(column, near, held, viewed(far_a))
    cross_late, weight, part = call(
        late_kernel, "late_pairs",
        [VMEM] * 13 + [ANY],
        [VMEM] * 3,
        [f32(CAP, SLAB_ROWS, LANES), f32(ROWS, LANES), f32(8, LANES)],
        [whole()] * 2
        + [pltpu.SMEM((6, BLOCK), jnp.float32)] * 3
        + [pltpu.SemaphoreType.DMA((1,)), pltpu.SemaphoreType.DMA((3,))],
    )(
        tile_blocks, shifts, column, side_a, side_b, near, held, cross_early, *sums,
        viewed(far_b),
    )

    def exchange(value):
        v = over_knot(value)
        me = (v[0] + v[1]) + (v[2] + v[3])
        third = move(jnp.pad(me, ((0, 24), (0, 0))), swap_c)
        both = jnp.concatenate([me, move(me, swap_a)], axis=0)
        ahead = move(both, same_d)
        third, ahead = lax.optimization_barrier((third, ahead))
        return both, ahead, third, move(ahead, swap_a)

    part, state, factor = call(
        step_kernel, "first_step",
        [VMEM] * 12,
        [VMEM] * 3,
        [f32(8, LANES), f32(8, LANES), f32(4 * BLOCK, LANES)],
        [whole(), square(), square()]
        + [pltpu.SMEM((6, BLOCK), jnp.float32), pltpu.SemaphoreType.DMA((1,))],
    )(
        tile_blocks, *exchange(part), column, side_a, side_b, start_coefficients, weight,
        cross_early, cross_late,
    )
    coef, warped = call(
        final_kernel, "second_step",
        [VMEM] * 8 + [ANY] * 2,
        [VMEM, ANY],
        [f32(1, BLOCK), f32(ROWS * DEPTH, LANES)],
        [pltpu.VMEM((ROWS * DEPTH, LANES), jnp.float32)] * 2
        + [pltpu.VMEM((ROWS, LANES), jnp.float32), square()]
        + [pltpu.SemaphoreType.DMA((2, CHUNKS)), pltpu.SemaphoreType.DMA((CHUNKS,))],
    )(tile_blocks, shifts, *exchange(part), state, factor, grad, image)
    warped = warped.reshape(ROWS, DEPTH, LANES).transpose(1, 0, 2).reshape(1, DEPTH, ROWS * LANES)
    return coef, warped


def solution(mesh):
    placed = (
        P("tile", "knot", None),
        P("tile", "knot", None),
        P("tile"),
        P("tile", None),
        P("tile", None, None, None),
        P(("tile", "knot"), None),
    )
    return jax.shard_map(
        per_device,
        mesh=mesh,
        in_specs=placed,
        out_specs=(P(("tile", "knot"), None), P("tile", "knot", None)),
        check_vma=False,
    )
```

```python
import functools

import jax
import jax.numpy as jnp
from jax import lax
from jax.experimental import pallas as pl
from jax.experimental.pallas import tpu as pltpu
from jax.sharding import PartitionSpec as P

SLAB = 8192
BLOCK = 64
LANES = 128
ROWS = 512
DEPTH = 8
LEAD = 16
PADDED = LEAD + ROWS + 16
GROUPS = SLAB // (8 * LANES) + 1
SLAB_ROWS = 8 * GROUPS
CAP = 8

shift_step = 0.05
smooth_weight = 20.0
ridge_weight = 1.0

EXACT = lax.Precision.HIGH


def iota(shape, dim):
    return lax.broadcasted_iota(jnp.int32, shape, dim)


def dot(a, b):
    return lax.dot_general(
        a, b, (((1,), (0,)), ((), ())), precision=EXACT, preferred_element_type=jnp.float32
    )


def dot_rows(a, b):
    return lax.dot_general(
        a, b, (((1,), (1,)), ((), ())), precision=EXACT, preferred_element_type=jnp.float32
    )


class Spline:
    def __init__(self):
        row = iota((ROWS, LANES), 0)
        lane = iota((ROWS, LANES), 1)
        self.low = (((row * LANES + lane) * 125) >> 16) == ((row * 125) >> 9)
        self.hot = (lane == ((row * 125) >> 9)).astype(jnp.float32)
        sub = iota((8, ROWS), 0)
        col = iota((8, ROWS), 1)
        first = (col * 125) >> 9
        centre = ((col * 256 + 127) * 125).astype(jnp.float32) * (1.0 / 131072.0)
        u = centre - first.astype(jnp.float32) - (sub >= 4).astype(jnp.float32)
        t = 1.0 - u
        k = 64.0 * 125.0 / 65536.0
        which = sub & 3
        def pick(a, b, c, d):
            return jnp.where(which == 0, a, jnp.where(which == 1, b, jnp.where(which == 2, c, d)))
        self.cubic = [
            pick(
                t * t * t / 6.0,
                2.0 / 3.0 - u * u + 0.5 * u * u * u,
                2.0 / 3.0 - t * t + 0.5 * t * t * t,
                u * u * u / 6.0,
            ),
            k * pick(-0.5 * t * t, -2.0 * u + 1.5 * u * u, 2.0 * t - 1.5 * t * t, 0.5 * u * u),
            (k * k) * pick(0.5 * t, 1.5 * u - 1.0, 1.5 * t - 1.0, 0.5 * u),
            (k * k * k) * pick(-1.0 / 6.0, 0.5, -0.5, 1.0 / 6.0),
        ]
        self.sub = sub
        eta = (iota((8, LANES), 1).astype(jnp.float32) - 63.5) * (1.0 / 64.0)
        power = iota((8, LANES), 0)
        q = jnp.ones((8, LANES), jnp.float32)
        for n in range(7):
            q = jnp.where(power > n, q * eta, q)
        self.powers = q

    def field(self, local):
        rows = [pltpu.roll(local, (LANES - s) % LANES, 1) if s else local for s in (0, 1, 2, 3)]
        rows += [pltpu.roll(local, LANES - s, 1) for s in (1, 2, 3, 4)]
        near = dot_rows(jnp.concatenate(rows, axis=0), self.hot)
        terms = jnp.concatenate([c * near for c in self.cubic], axis=0)
        wide = iota((32, 2 * LANES), 1)
        high = (iota((32, 2 * LANES), 0) & 4) != 0
        order = iota((32, 2 * LANES), 0) >> 3
        eta = ((wide & 127).astype(jnp.float32) - 63.5) * (1.0 / 64.0)
        power = jnp.where(
            order == 0, 1.0, jnp.where(order == 1, eta, jnp.where(order == 2, eta * eta, eta * eta * eta))
        )
        power = jnp.where(high == (wide >= LANES), power, 0.0)
        both = dot(terms.T, power)
        return jnp.where(self.low, both[:, :LANES], both[:, LANES:])

    def moments(self, value):
        low = jnp.where(self.low, value, 0.0)
        high = jnp.where(self.low, 0.0, value)
        a = dot_rows(self.powers, low)
        b = dot_rows(self.powers, high)
        return lambda n: jnp.where(self.sub < 4, a[n : n + 1], b[n : n + 1])

    def gather(self, rows):
        total = rows[0:1]
        for s in range(1, 4):
            total = total + pltpu.roll(rows[s : s + 1], s, 1)
        for s in range(4):
            total = total + pltpu.roll(rows[4 + s : 5 + s], s + 1, 1)
        return total

    def sums(self, value):
        part = self.moments(value)
        return sum(self.cubic[n] * part(n) for n in range(4))

    def adjoints(self, values, weight=None):
        stack = [self.sums(v) for v in values]
        if weight is not None:
            stack += self.bands(weight)
        rows = dot(jnp.concatenate(stack, axis=0), self.hot)
        return [self.gather(rows[8 * n : 8 * n + 8]) for n in range(len(stack))]

    def bands(self, value):
        part = self.moments(value)
        parts = [part(n) for n in range(7)]
        y = [sum(self.cubic[j] * parts[i + j] for j in range(4)) for i in range(4)]
        stack = []
        for m in range(4):
            moved = [pltpu.roll(v, 8 - m, 0) if m else v for v in y]
            rows = sum(self.cubic[i] * moved[i] for i in range(4))
            stack.append(jnp.where((self.sub & 3) + m < 4, rows, 0.0))
        return stack


LAST_ROW = ROWS - SLAB_ROWS


class Here:
    def __init__(self, blocks=None, shifts=None):
        self.tile = lax.axis_index("tile").astype(jnp.int32)
        self.knot = lax.axis_index("knot").astype(jnp.int32)
        odd = self.tile & 1
        self.to_a = jnp.where(odd == 0, 2, 0)
        self.to_b = 2 - self.to_a
        self.side_b = self.tile + jnp.where(odd == 0, -1, 1)
        if blocks is not None:
            both = blocks[...].astype(jnp.float32)
            self.blocks = [jnp.broadcast_to(both[:, n : n + 1], (1, LANES)) for n in range(2)]
        if shifts is not None:
            self.rigid = shift_step * jnp.broadcast_to(
                shifts[...].astype(jnp.float32), (1, LANES)
            )

    def block_row(self):
        lane = iota((1, LANES), 1)
        row = jnp.where(lane < BLOCK, self.blocks[0], self.blocks[1])
        return jnp.where(self.knot == 0, 1.0, 0.0) * row

    def block_ids(self):
        owned = (self.tile * 4 + self.knot).astype(jnp.float32)
        return self.blocks + [jnp.full((1, LANES), owned)]


def place(pair, p):
    off_b, off_a = pair(p, 1), pair(p, 3)
    row_b = jnp.minimum(off_b >> 7, LAST_ROW)
    lead = off_b - row_b * LANES
    start = off_a - lead
    return row_b, lead, start >> 7, start & 127


def window(ref, row, rows=SLAB_ROWS):
    return ref.at[pl.ds(pl.multiple_of((row + LEAD) * 8, 8), rows * 8)]


def rows_at(row, plane):
    return pl.ds(row * 8 + plane, 8, stride=8)


def all_rows(plane, back=0):
    return pl.ds((LEAD - back) * 8 + plane, ROWS, stride=8)


def moved_sums(planes, plane, row_a, turn, values):
    keep = iota((8, LANES), 1) >= turn
    out = window(planes, row_a)
    sums = []
    for i, value in enumerate(values):
        moved = pltpu.roll(value, turn, 1)
        sums.append(
            (
                out[rows_at(8 * i, plane), :] + jnp.where(keep, moved, 0.0),
                out[rows_at(8 * i, plane + 1), :] + jnp.where(keep, 0.0, moved),
            )
        )

    def store():
        for i, (kept, passed) in enumerate(sums):
            out[rows_at(8 * i, plane), :] = kept
            out[rows_at(8 * i, plane + 1), :] = passed

    return store


def live_count(pair):
    total = pair(0, 4)
    for p in range(1, CAP):
        total = total + pair(p, 4)
    return total


def sent_reader(ref, direction):
    def read(p, field):
        at = (direction * CAP + p) * 5 + field
        return ref[4 + (at >> 6), at & 63].astype(jnp.int32)

    return read


FIELD, COUNT = 6, 7


def slabs(pair, base, far, grad, image, cross, planes, plane, with_field):
    lane = iota((8, LANES), 1)
    sub = iota((8, LANES), 0)

    def body(p, carry):
        row_b, lead, row_a, turn = place(pair, p)
        back = (LANES - turn) & 127
        keep = lane >= turn
        values = []
        far_rows = window(far, row_a, SLAB_ROWS + 8)
        grad_rows = window(grad, row_b)
        image_rows = window(image, row_b)
        field_rows = window(planes, row_b)
        for i in range(GROUPS):
            c = jnp.zeros((8, LANES), jnp.float32)
            x = jnp.zeros((8, LANES), jnp.float32)
            for z in range(DEPTH):
                first = far_rows[rows_at(8 * i, z), :]
                second = far_rows[rows_at(8 * i + 1, z), :]
                slope = pltpu.roll(jnp.where(keep, first, second), back, 1)
                c = c + slope * grad_rows[rows_at(8 * i, z), :]
                x = x + slope * image_rows[rows_at(8 * i, z), :]
            if i in (0, 1, GROUPS - 1):
                s = (sub + 8 * i) * LANES + lane - lead
                valid = (s >= 0) & (s < SLAB)
                c = jnp.where(valid, c, 0.0)
                x = jnp.where(valid, x, 0.0)
            cross[base + p, 8 * i : 8 * i + 8, :] = c
            if with_field:
                x = x + c * field_rows[rows_at(8 * i, FIELD), :]
            values.append(x)
        moved_sums(planes, plane, row_a, turn, values)()
        return carry

    lax.fori_loop(0, live_count(pair), body, 0)


def slab_steps(groups, planes):
    counts = [live_count(pair) for pair, _, _, _ in groups]
    total = functools.reduce(jnp.maximum, counts)

    def body(p, carry):
        done = []
        for (pair, base, cross, plane), count in zip(groups, counts):
            row_b, _, row_a, turn = place(pair, p)
            field_rows = window(planes, row_b)
            live = p < count
            values = [
                jnp.where(
                    live,
                    cross[base + p, 8 * i : 8 * i + 8, :] * field_rows[rows_at(8 * i, FIELD), :],
                    0.0,
                )
                for i in range(GROUPS)
            ]
            done.append(moved_sums(planes, plane, row_a, turn, values))
        for store in done:
            store()
        return carry

    lax.fori_loop(0, total, body, 0)


def collected(planes, plane):
    return planes[all_rows(plane), :] + planes[all_rows(plane + 1, 1), :]


def clear(refs):
    for ref in refs:
        ref[...] = jnp.zeros(ref.shape, jnp.float32)


def clear_ends(ref):
    ref[0 : LEAD * 8, :] = jnp.zeros((LEAD * 8, LANES), jnp.float32)
    ref[(LEAD + ROWS) * 8 :, :] = jnp.zeros(((PADDED - LEAD - ROWS) * 8, LANES), jnp.float32)


def local_values(here, tables):
    out = [jnp.zeros((1, BLOCK), jnp.float32) for _ in range(2)]
    for table, col in zip(tables, (here.tile, here.tile ^ 1, here.side_b)):
        for n in range(4):
            held = (col * 4 + ((here.knot - n) & 3)).astype(jnp.float32)
            for half in range(2):
                out[half] = jnp.where(
                    here.blocks[half][:, :BLOCK] == held, table[n : n + 1, :], out[half]
                )
    return jnp.concatenate(out, axis=1)


def scalar_copies(tables, scalars, sems):
    copies = [
        pltpu.make_async_copy(t, m, sems.at[n]) for n, (t, m) in enumerate(zip(tables, scalars))
    ]
    for c in copies:
        c.start()
    return copies


def padded_copy(source, target, sem):
    return pltpu.make_async_copy(source, target.at[pl.ds(LEAD * 8, ROWS * 8)], sem)


def cover(pair, planes):
    lane = iota((8, LANES), 1)
    sub = iota((8, LANES), 0)

    def body(p, carry):
        off = pair(p, 3)
        rows = window(planes, off >> 7)
        counts = [rows[rows_at(8 * i, COUNT), :] for i in range(GROUPS)]
        for i in range(GROUPS):
            s = (sub + 8 * i) * LANES + lane - (off & 127)
            inside = (s >= 0) & (s < SLAB)
            rows[rows_at(8 * i, COUNT), :] = counts[i] + jnp.where(inside, 1.0, 0.0)
        return carry

    lax.fori_loop(0, live_count(pair), body, 0)


def early_kernel(
    column, near, image, far_in,
    cross, weight_out, value_out, own_out, side_out, count_out,
    far, planes, scalars, sems,
):
    reads = scalar_copies((column,), (scalars,), sems)
    copy = padded_copy(far_in, far, sems.at[1])
    copy.start()
    clear_ends(far)
    clear((planes,))
    here = Here()

    def rows(g, carry):
        w = jnp.zeros((8, LANES), jnp.float32)
        v = jnp.zeros((8, LANES), jnp.float32)
        for z in range(DEPTH):
            slope = near[pl.ds(64 * g + (LEAD * 8 + z), 8, stride=8), :]
            w = w + slope * slope
            v = v + slope * image[pl.ds(64 * g + (LEAD * 8 + z), 8, stride=8), :]
        at = pl.ds(pl.multiple_of(8 * g, 8), 8)
        weight_out[at, :] = w
        value_out[at, :] = v
        return carry

    lax.fori_loop(0, ROWS // 8, rows, 0)
    reads[0].wait()
    cover(sent_reader(scalars, 1), planes)
    slabs(sent_reader(scalars, 1), 0, near, near, image, cross, planes, 0, False)
    copy.wait()
    slabs(sent_reader(scalars, here.to_a), CAP, far, near, image, cross, planes, 2, False)
    own_out[...] = collected(planes, 0)
    side_out[...] = collected(planes, 2)
    count_out[...] = planes[all_rows(COUNT), :]


def late_kernel(
    blocks, shifts, column, side_a, side_b,
    near, image, cross_early, weight, value, own, side, counted, far_in,
    cross, weight_out, part_out,
    far, planes, scalars_own, scalars_a, scalars_b, sems, scalar_sems,
):
    reads = scalar_copies(
        (column, side_a, side_b), (scalars_own, scalars_a, scalars_b), scalar_sems
    )
    copy = padded_copy(far_in, far, sems.at[0])
    copy.start()
    here = Here(blocks, shifts)
    clear_ends(far)
    clear((planes,))
    spline = Spline()
    field = spline.field(local_values(here, (column, side_a, side_b))) + here.rigid
    planes[all_rows(FIELD), :] = field
    for c in reads:
        c.wait()
    cover(sent_reader(scalars_a, 2 - here.to_a), planes)
    cover(sent_reader(scalars_b, 2 - here.to_b), planes)
    slab_steps(
        [
            (sent_reader(scalars_own, 1), 0, cross_early, 0),
            (sent_reader(scalars_own, here.to_a), CAP, cross_early, 2),
        ],
        planes,
    )
    copy.wait()
    slabs(sent_reader(scalars_own, here.to_b), 0, far, near, image, cross, planes, 4, True)
    n = counted[...] + planes[all_rows(COUNT), :]
    w = weight[...] * n
    weight_out[...] = w
    mine = value[...] * n + w * planes[all_rows(FIELD), :] - own[...] - collected(planes, 0)
    others = [side[...] + collected(planes, 2), collected(planes, 4)]
    rows = spline.adjoints([mine] + others, w)
    part_out[0:1, :] = rows[0]
    part_out[1:2, :] = -rows[1]
    part_out[2:3, :] = -rows[2]
    part_out[3:4, :] = here.block_row()
    for m in range(4):
        part_out[4 + m : 5 + m, :] = rows[3 + m]


def near_tiles(both, ahead, third, behind):
    me, a = both[0:8, :], both[8:16, :]
    d, b = ahead[0:8, :], ahead[8:16, :]
    sd, sb = behind[0:8, :], behind[8:16, :]
    c = third[0:8, :]
    return [
        (me, me[0:1] + a[1:2] + b[2:3]),
        (a, a[0:1] + me[1:2] + sb[2:3]),
        (b, b[0:1] + d[1:2] + me[2:3]),
        (d, d[0:1] + b[1:2] + c[2:3]),
        (sb, sb[0:1] + sd[1:2] + a[2:3]),
    ]


def folded(rows):
    return rows + pltpu.roll(rows, BLOCK, 1)


def block_sums(tiles, block):
    total = jnp.zeros((1, LANES), jnp.float32)
    for ref, grad in tiles:
        total = total + jnp.where(ref[3:4] == block, grad, 0.0)
    lane = iota((1, LANES), 1)
    return jnp.where(lane < BLOCK, folded(total), 0.0)


def pulled(coef):
    lane = iota((1, LANES), 1)
    y = coef - 2.0 * pltpu.roll(coef, LANES - 1, 1) + pltpu.roll(coef, LANES - 2, 1)
    y = jnp.where(lane < BLOCK - 2, y, 0.0)
    return jnp.where(lane < BLOCK, y - 2.0 * pltpu.roll(y, 1, 1) + pltpu.roll(y, 2, 1), 0.0)


def solve(target, factor, steps):
    y = []
    for i in range(BLOCK):
        v = target[i : i + 1, :]
        for j in range(1, 4):
            if i >= j:
                v = v - factor[j * BLOCK + i - j : j * BLOCK + i - j + 1, :] * y[i - j]
        y.append(v)
    x = [None] * BLOCK
    for i in reversed(range(BLOCK)):
        v = y[i] * factor[i : i + 1, :]
        for j in range(3, 0, -1):
            if i + j < BLOCK:
                v = v - factor[j * BLOCK + i : j * BLOCK + i + 1, :] * x[i + j]
        x[i] = v
        steps[i : i + 1, :] = v


def across(rows):
    block = jnp.concatenate(rows + [jnp.zeros((LANES - len(rows), LANES), jnp.float32)], axis=0)
    return block.T


def joined(coefs):
    lane = iota((1, LANES), 1)
    return jnp.where(lane < BLOCK, coefs[0], pltpu.roll(coefs[1], BLOCK, 1))


def step_kernel(
    blocks, both, ahead, third, behind, column, side_a, side_b, start, weight,
    cross_early, cross_late,
    part_out, state, factor,
    planes, steps, work, scalars, scalar_sems,
):
    reads = scalar_copies((column,), (scalars,), scalar_sems)
    here = Here(blocks)
    clear((planes, steps))
    lane = iota((1, LANES), 1)
    zero = jnp.zeros((1, LANES), jnp.float32)
    tiles = near_tiles(both, ahead, third, behind)
    knots = local_values(here, (column, side_a, side_b))
    coefs = [
        jnp.where(lane < BLOCK, knots, 0.0),
        jnp.where(lane < BLOCK, pltpu.roll(knots, BLOCK, 1), 0.0),
        jnp.concatenate([start[...], jnp.zeros((1, LANES - BLOCK), jnp.float32)], axis=1),
    ]
    sums = []
    rows = []
    for q, block in enumerate(here.block_ids()):
        gradsum = block_sums(tiles, block)
        sums.append(gradsum)
        bands = []
        for m in range(4):
            total = zero
            for ref, _ in tiles:
                total = total + jnp.where(ref[3:4] == block, ref[4 + m : 5 + m], 0.0)
            total = jnp.where((lane & (BLOCK - 1)) + m < BLOCK, total, 0.0)
            bands.append(folded(total))
        inside = lambda cond: jnp.where(cond, 1.0, 0.0)
        upper, lower = inside(lane < BLOCK - 2), inside(lane >= 2)
        middle = inside((lane >= 1) & (lane < BLOCK - 1))
        bands[0] = bands[0] + smooth_weight * (upper + 4.0 * middle + lower) + ridge_weight
        bands[1] = bands[1] - smooth_weight * 2.0 * (
            upper + inside((lane >= 1) & (lane < BLOCK - 1))
        )
        bands[2] = bands[2] + smooth_weight * upper
        target = -(gradsum + smooth_weight * pulled(coefs[q]))
        rows += bands + [target, zero, zero, zero]
    work[...] = across(rows)
    turned = [work[0:BLOCK, :]] + [pltpu.roll(work[0:BLOCK, :], LANES - m, 1) for m in range(1, 5)]
    band = [[turned[m][i : i + 1, :] for i in range(BLOCK)] for m in range(4)]
    for i in range(BLOCK):
        r = 1.0 / band[0][i]
        factor[i : i + 1, :] = r
        cs = [band[m][i] for m in range(1, 4)]
        ls = [v * r for v in cs]
        for j in range(1, 4):
            factor[j * BLOCK + i : j * BLOCK + i + 1, :] = ls[j - 1]
            if i + j < BLOCK:
                for m in range(0, 4 - j):
                    band[m][i + j] = band[m][i + j] - ls[j - 1] * cs[j - 1 + m]
    solve(turned[4], factor, steps)
    moved = steps[...].T
    change = [moved[8 * q : 8 * q + 1, :] for q in range(3)]
    state[...] = jnp.concatenate(
        [coefs[q] + change[q] for q in range(3)] + [zero] + sums + [zero], axis=0
    )
    spline = Spline()
    planes[all_rows(FIELD), :] = spline.field(joined(change))
    reads[0].wait()
    slab_steps(
        [
            (sent_reader(scalars, 1), 0, cross_early, 0),
            (sent_reader(scalars, here.to_a), CAP, cross_early, 2),
            (sent_reader(scalars, here.to_b), 0, cross_late, 4),
        ],
        planes,
    )
    mine = weight[...] * planes[all_rows(FIELD), :] - collected(planes, 0)
    rows = spline.adjoints([mine, collected(planes, 2), collected(planes, 4)])
    part_out[0:1, :] = rows[0]
    part_out[1:2, :] = -rows[1]
    part_out[2:3, :] = -rows[2]
    part_out[3:4, :] = here.block_row()
    part_out[4:8, :] = jnp.zeros((4, LANES), jnp.float32)


CHUNKS = 8


def final_kernel(
    blocks, shifts, both, ahead, third, behind, state, factor, grad_in, image_in,
    coef_out, warped_out,
    grad, image, field, steps, sems, out_sems,
):
    size = ROWS * 8 // CHUNKS
    at = [pl.ds(n * size, size) for n in range(CHUNKS)]
    loads = []
    for n in range(CHUNKS):
        loads.append(pltpu.make_async_copy(grad_in.at[at[n]], grad.at[at[n]], sems.at[0, n]))
        loads.append(pltpu.make_async_copy(image_in.at[at[n]], image.at[at[n]], sems.at[1, n]))
    for copy in loads:
        copy.start()
    here = Here(blocks, shifts)
    steps[...] = jnp.zeros((LANES, LANES), jnp.float32)
    tiles = near_tiles(both, ahead, third, behind)
    zero = jnp.zeros((1, LANES), jnp.float32)
    coefs = [state[q : q + 1, :] for q in range(3)]
    rows = []
    for q, block in enumerate(here.block_ids()):
        gradsum = state[4 + q : 5 + q, :] + block_sums(tiles, block)
        rows += [-(gradsum + smooth_weight * pulled(coefs[q]))] + [zero] * 7
    solve(across(rows)[0:BLOCK, :], factor, steps)
    moved = steps[...].T
    coefs = [coefs[q] + moved[8 * q : 8 * q + 1, :] for q in range(3)]
    coef_out[...] = coefs[2][:, :BLOCK]
    spline = Spline()
    field[...] = spline.field(joined(coefs)) + here.rigid
    stores = []
    for n in range(CHUNKS):
        loads[2 * n].wait()
        loads[2 * n + 1].wait()

        def body(g, carry):
            for r in range(8):
                row = g * 8 + r
                rows = pl.ds(pl.multiple_of(row * 8, 8), 8)
                image[rows, :] = image[rows, :] + grad[rows, :] * field[pl.ds(row, 1), :]
            return carry

        lax.fori_loop(n * size // 64, (n + 1) * size // 64, body, 0)
        stores.append(pltpu.make_async_copy(image.at[at[n]], warped_out.at[at[n]], out_sems.at[n]))
        stores[-1].start()
    for copy in stores:
        copy.wait()


VMEM = pl.BlockSpec(memory_space=pltpu.VMEM)
ANY = pl.BlockSpec(memory_space=pl.ANY)
HBM = pl.BlockSpec(memory_space=pltpu.HBM)


def f32(*shape):
    return jax.ShapeDtypeStruct(shape, jnp.float32)


def call(kernel, name, in_specs, out_specs, out_shape, scratch):
    return pl.pallas_call(
        kernel,
        name=name,
        in_specs=in_specs,
        out_specs=out_specs,
        out_shape=out_shape,
        scratch_shapes=scratch,
        compiler_params=pltpu.CompilerParams(vmem_limit_bytes=24 * 1024 * 1024),
    )


def whole():
    return pltpu.VMEM((PADDED * 8, LANES), jnp.float32)


def square():
    return pltpu.VMEM((LANES, LANES), jnp.float32)


def viewed(block):
    return block.reshape(DEPTH, ROWS, LANES).transpose(1, 0, 2).reshape(ROWS * DEPTH, LANES)


def per_device(images, gradient, shifts, tile_blocks, intersections, start_coefficients):
    tiles = lax.axis_size("tile")
    knots = lax.axis_size("knot")
    ids = range(tiles)
    swap_a = [(i, i ^ 1) for i in ids]
    swap_b = [(i, ((i - 1) ^ 1) + 1) for i in ids if 0 < i < tiles - 1]
    swap_c = [(i, i + 3 if i % 2 else i - 3) for i in ids]
    swap_c = [(i, j) for i, j in swap_c if 0 <= j < tiles]
    same_d = [(i, i + 2 if i % 2 == 0 else i - 2) for i in ids]
    same_d = [(i, j) for i, j in same_d if 0 <= j < tiles]

    def move(value, route):
        return lax.ppermute(value, "tile", route)

    def over_knot(value):
        return [value] + [
            lax.ppermute(value, "knot", [(i, (i + s) % knots) for i in range(knots)])
            for s in range(1, knots)
        ]

    shifts = shifts.reshape(1, 1)
    far_b = move(gradient, swap_b)
    far_a = move(gradient, swap_a)
    sent = jnp.pad(intersections.reshape(1, -1).astype(jnp.float32), ((0, 0), (0, 8)))
    column = jnp.concatenate(over_knot(start_coefficients) + [sent.reshape(2, BLOCK)], axis=0)
    side_a, side_b = move(column, swap_a), move(column, swap_b)

    grad, image = viewed(gradient), viewed(images)
    ends = ((LEAD * 8, (PADDED - LEAD - ROWS) * 8), (0, 0))
    near, held = jnp.pad(grad, ends), jnp.pad(image, ends)
    cross_early, *sums = call(
        early_kernel, "early_pairs",
        [VMEM] * 3 + [HBM],
        [VMEM] * 6,
        [f32(2 * CAP, SLAB_ROWS, LANES)] + [f32(ROWS, LANES)] * 5,
        [whole()] * 2 + [pltpu.SMEM((6, BLOCK), jnp.float32), pltpu.SemaphoreType.DMA((2,))],
    )(column, near, held, viewed(far_a))
    cross_late, weight, part = call(
        late_kernel, "late_pairs",
        [VMEM] * 13 + [ANY],
        [VMEM] * 3,
        [f32(CAP, SLAB_ROWS, LANES), f32(ROWS, LANES), f32(8, LANES)],
        [whole()] * 2
        + [pltpu.SMEM((6, BLOCK), jnp.float32)] * 3
        + [pltpu.SemaphoreType.DMA((1,)), pltpu.SemaphoreType.DMA((3,))],
    )(
        tile_blocks, shifts, column, side_a, side_b, near, held, cross_early, *sums,
        viewed(far_b),
    )

    def exchange(value):
        v = over_knot(value)
        me = (v[0] + v[1]) + (v[2] + v[3])
        third = move(jnp.pad(me, ((0, 24), (0, 0))), swap_c)
        both = jnp.concatenate([me, move(me, swap_a)], axis=0)
        ahead = move(both, same_d)
        third, ahead = lax.optimization_barrier((third, ahead))
        return both, ahead, third, move(ahead, swap_a)

    part, state, factor = call(
        step_kernel, "first_step",
        [VMEM] * 12,
        [VMEM] * 3,
        [f32(8, LANES), f32(8, LANES), f32(4 * BLOCK, LANES)],
        [whole(), square(), square()]
        + [pltpu.SMEM((6, BLOCK), jnp.float32), pltpu.SemaphoreType.DMA((1,))],
    )(
        tile_blocks, *exchange(part), column, side_a, side_b, start_coefficients, weight,
        cross_early, cross_late,
    )
    coef, warped = call(
        final_kernel, "second_step",
        [VMEM] * 8 + [ANY] * 2,
        [VMEM, ANY],
        [f32(1, BLOCK), f32(ROWS * DEPTH, LANES)],
        [pltpu.VMEM((ROWS * DEPTH, LANES), jnp.float32)] * 2
        + [pltpu.VMEM((ROWS, LANES), jnp.float32), square()]
        + [pltpu.SemaphoreType.DMA((2, CHUNKS)), pltpu.SemaphoreType.DMA((CHUNKS,))],
    )(tile_blocks, shifts, *exchange(part), state, factor, grad, image)
    warped = warped.reshape(ROWS, DEPTH, LANES).transpose(1, 0, 2).reshape(1, DEPTH, ROWS * LANES)
    return coef, warped


def solution(mesh):
    placed = (
        P("tile", "knot", None),
        P("tile", "knot", None),
        P("tile"),
        P("tile", None),
        P("tile", None, None, None),
        P(("tile", "knot"), None),
    )
    return jax.shard_map(
        per_device,
        mesh=mesh,
        in_specs=placed,
        out_specs=(P(("tile", "knot"), None), P("tile", "knot", None)),
        check_vma=False,
    )
```

```python
import functools

import jax
import jax.numpy as jnp
from jax import lax
from jax.experimental import pallas as pl
from jax.experimental.pallas import tpu as pltpu
from jax.sharding import PartitionSpec as P

SLAB = 8192
BLOCK = 64
LANES = 128
ROWS = 512
DEPTH = 8
LEAD = 16
PADDED = LEAD + ROWS + 16
GROUPS = SLAB // (8 * LANES) + 1
SLAB_ROWS = 8 * GROUPS
CAP = 8

shift_step = 0.05
smooth_weight = 20.0
ridge_weight = 1.0

EXACT = lax.Precision.HIGH


def iota(shape, dim):
    return lax.broadcasted_iota(jnp.int32, shape, dim)


def dot(a, b):
    return lax.dot_general(
        a, b, (((1,), (0,)), ((), ())), precision=EXACT, preferred_element_type=jnp.float32
    )


def dot_rows(a, b):
    return lax.dot_general(
        a, b, (((1,), (1,)), ((), ())), precision=EXACT, preferred_element_type=jnp.float32
    )


class Spline:
    def __init__(self):
        row = iota((ROWS, LANES), 0)
        lane = iota((ROWS, LANES), 1)
        self.low = (((row * LANES + lane) * 125) >> 16) == ((row * 125) >> 9)
        self.hot = (lane == ((row * 125) >> 9)).astype(jnp.float32)
        sub = iota((8, ROWS), 0)
        col = iota((8, ROWS), 1)
        first = (col * 125) >> 9
        centre = ((col * 256 + 127) * 125).astype(jnp.float32) * (1.0 / 131072.0)
        u = centre - first.astype(jnp.float32) - (sub >= 4).astype(jnp.float32)
        t = 1.0 - u
        k = 64.0 * 125.0 / 65536.0
        which = sub & 3
        def pick(a, b, c, d):
            return jnp.where(which == 0, a, jnp.where(which == 1, b, jnp.where(which == 2, c, d)))
        self.cubic = [
            pick(
                t * t * t / 6.0,
                2.0 / 3.0 - u * u + 0.5 * u * u * u,
                2.0 / 3.0 - t * t + 0.5 * t * t * t,
                u * u * u / 6.0,
            ),
            k * pick(-0.5 * t * t, -2.0 * u + 1.5 * u * u, 2.0 * t - 1.5 * t * t, 0.5 * u * u),
            (k * k) * pick(0.5 * t, 1.5 * u - 1.0, 1.5 * t - 1.0, 0.5 * u),
            (k * k * k) * pick(-1.0 / 6.0, 0.5, -0.5, 1.0 / 6.0),
        ]
        self.sub = sub
        eta = (iota((8, LANES), 1).astype(jnp.float32) - 63.5) * (1.0 / 64.0)
        power = iota((8, LANES), 0)
        q = jnp.ones((8, LANES), jnp.float32)
        for n in range(7):
            q = jnp.where(power > n, q * eta, q)
        self.powers = q

    def field(self, local):
        rows = [pltpu.roll(local, (LANES - s) % LANES, 1) if s else local for s in (0, 1, 2, 3)]
        rows += [pltpu.roll(local, LANES - s, 1) for s in (1, 2, 3, 4)]
        near = dot_rows(jnp.concatenate(rows, axis=0), self.hot)
        terms = jnp.concatenate([c * near for c in self.cubic], axis=0)
        wide = iota((32, 2 * LANES), 1)
        high = (iota((32, 2 * LANES), 0) & 4) != 0
        order = iota((32, 2 * LANES), 0) >> 3
        eta = ((wide & 127).astype(jnp.float32) - 63.5) * (1.0 / 64.0)
        power = jnp.where(
            order == 0, 1.0, jnp.where(order == 1, eta, jnp.where(order == 2, eta * eta, eta * eta * eta))
        )
        power = jnp.where(high == (wide >= LANES), power, 0.0)
        both = dot(terms.T, power)
        return jnp.where(self.low, both[:, :LANES], both[:, LANES:])

    def moments(self, value):
        low = jnp.where(self.low, value, 0.0)
        high = jnp.where(self.low, 0.0, value)
        a = dot_rows(self.powers, low)
        b = dot_rows(self.powers, high)
        return lambda n: jnp.where(self.sub < 4, a[n : n + 1], b[n : n + 1])

    def gather(self, rows):
        total = rows[0:1]
        for s in range(1, 4):
            total = total + pltpu.roll(rows[s : s + 1], s, 1)
        for s in range(4):
            total = total + pltpu.roll(rows[4 + s : 5 + s], s + 1, 1)
        return total

    def sums(self, value):
        part = self.moments(value)
        return sum(self.cubic[n] * part(n) for n in range(4))

    def adjoints(self, values, weight=None):
        stack = [self.sums(v) for v in values]
        if weight is not None:
            stack += self.bands(weight)
        rows = dot(jnp.concatenate(stack, axis=0), self.hot)
        return [self.gather(rows[8 * n : 8 * n + 8]) for n in range(len(stack))]

    def bands(self, value):
        part = self.moments(value)
        parts = [part(n) for n in range(7)]
        y = [sum(self.cubic[j] * parts[i + j] for j in range(4)) for i in range(4)]
        stack = []
        for m in range(4):
            moved = [pltpu.roll(v, 8 - m, 0) if m else v for v in y]
            rows = sum(self.cubic[i] * moved[i] for i in range(4))
            stack.append(jnp.where((self.sub & 3) + m < 4, rows, 0.0))
        return stack


LAST_ROW = ROWS - SLAB_ROWS


class Here:
    def __init__(self, blocks=None, shifts=None):
        self.tile = lax.axis_index("tile").astype(jnp.int32)
        self.knot = lax.axis_index("knot").astype(jnp.int32)
        odd = self.tile & 1
        self.to_a = jnp.where(odd == 0, 2, 0)
        self.to_b = 2 - self.to_a
        self.side_b = self.tile + jnp.where(odd == 0, -1, 1)
        if blocks is not None:
            both = blocks[...].astype(jnp.float32)
            self.blocks = [jnp.broadcast_to(both[:, n : n + 1], (1, LANES)) for n in range(2)]
        if shifts is not None:
            self.rigid = shift_step * jnp.broadcast_to(
                shifts[...].astype(jnp.float32), (1, LANES)
            )

    def block_row(self):
        lane = iota((1, LANES), 1)
        row = jnp.where(lane < BLOCK, self.blocks[0], self.blocks[1])
        return jnp.where(self.knot == 0, 1.0, 0.0) * row

    def block_ids(self):
        owned = (self.tile * 4 + self.knot).astype(jnp.float32)
        return self.blocks + [jnp.full((1, LANES), owned)]


def place(pair, p):
    off_b, off_a = pair(p, 1), pair(p, 3)
    row_b = jnp.minimum(off_b >> 7, LAST_ROW)
    lead = off_b - row_b * LANES
    start = off_a - lead
    return row_b, lead, start >> 7, start & 127


def window(ref, row, rows=SLAB_ROWS):
    return ref.at[pl.ds(pl.multiple_of((row + LEAD) * 8, 8), rows * 8)]


def rows_at(row, plane):
    return pl.ds(row * 8 + plane, 8, stride=8)


def all_rows(plane, back=0):
    return pl.ds((LEAD - back) * 8 + plane, ROWS, stride=8)


def moved_sums(planes, plane, row_a, turn, values):
    keep = iota((8, LANES), 1) >= turn
    out = window(planes, row_a)
    sums = []
    for i, value in enumerate(values):
        moved = pltpu.roll(value, turn, 1)
        sums.append(
            (
                out[rows_at(8 * i, plane), :] + jnp.where(keep, moved, 0.0),
                out[rows_at(8 * i, plane + 1), :] + jnp.where(keep, 0.0, moved),
            )
        )

    def store():
        for i, (kept, passed) in enumerate(sums):
            out[rows_at(8 * i, plane), :] = kept
            out[rows_at(8 * i, plane + 1), :] = passed

    return store


def live_count(pair):
    total = pair(0, 4)
    for p in range(1, CAP):
        total = total + pair(p, 4)
    return total


def sent_reader(ref, direction):
    def read(p, field):
        at = (direction * CAP + p) * 5 + field
        return ref[4 + (at >> 6), at & 63].astype(jnp.int32)

    return read


FIELD, COUNT = 6, 7


def slabs(pair, base, far, grad, image, cross, planes, plane, with_field):
    lane = iota((8, LANES), 1)
    sub = iota((8, LANES), 0)

    def body(p, carry):
        row_b, lead, row_a, turn = place(pair, p)
        back = (LANES - turn) & 127
        keep = lane >= turn
        values = []
        far_rows = window(far, row_a, SLAB_ROWS + 8)
        grad_rows = window(grad, row_b)
        image_rows = window(image, row_b)
        field_rows = window(planes, row_b)
        for i in range(GROUPS):
            c = jnp.zeros((8, LANES), jnp.float32)
            x = jnp.zeros((8, LANES), jnp.float32)
            for z in range(DEPTH):
                first = far_rows[rows_at(8 * i, z), :]
                second = far_rows[rows_at(8 * i + 1, z), :]
                slope = pltpu.roll(jnp.where(keep, first, second), back, 1)
                c = c + slope * grad_rows[rows_at(8 * i, z), :]
                x = x + slope * image_rows[rows_at(8 * i, z), :]
            if i in (0, 1, GROUPS - 1):
                s = (sub + 8 * i) * LANES + lane - lead
                valid = (s >= 0) & (s < SLAB)
                c = jnp.where(valid, c, 0.0)
                x = jnp.where(valid, x, 0.0)
            cross[base + p, 8 * i : 8 * i + 8, :] = c
            if with_field:
                x = x + c * field_rows[rows_at(8 * i, FIELD), :]
            values.append(x)
        moved_sums(planes, plane, row_a, turn, values)()
        return carry

    lax.fori_loop(0, live_count(pair), body, 0)


def slab_steps(groups, planes):
    counts = [live_count(pair) for pair, _, _, _ in groups]
    total = functools.reduce(jnp.maximum, counts)

    def body(p, carry):
        done = []
        for (pair, base, cross, plane), count in zip(groups, counts):
            row_b, _, row_a, turn = place(pair, p)
            field_rows = window(planes, row_b)
            live = p < count
            values = [
                jnp.where(
                    live,
                    cross[base + p, 8 * i : 8 * i + 8, :] * field_rows[rows_at(8 * i, FIELD), :],
                    0.0,
                )
                for i in range(GROUPS)
            ]
            done.append(moved_sums(planes, plane, row_a, turn, values))
        for store in done:
            store()
        return carry

    lax.fori_loop(0, total, body, 0)


def collected(planes, plane):
    return planes[all_rows(plane), :] + planes[all_rows(plane + 1, 1), :]


def clear(refs):
    for ref in refs:
        ref[...] = jnp.zeros(ref.shape, jnp.float32)


def clear_ends(ref):
    ref[0 : LEAD * 8, :] = jnp.zeros((LEAD * 8, LANES), jnp.float32)
    ref[(LEAD + ROWS) * 8 :, :] = jnp.zeros(((PADDED - LEAD - ROWS) * 8, LANES), jnp.float32)


def local_values(here, tables):
    out = [jnp.zeros((1, BLOCK), jnp.float32) for _ in range(2)]
    for table, col in zip(tables, (here.tile, here.tile ^ 1, here.side_b)):
        for n in range(4):
            held = (col * 4 + ((here.knot - n) & 3)).astype(jnp.float32)
            for half in range(2):
                out[half] = jnp.where(
                    here.blocks[half][:, :BLOCK] == held, table[n : n + 1, :], out[half]
                )
    return jnp.concatenate(out, axis=1)


def scalar_copies(tables, scalars, sems):
    copies = [
        pltpu.make_async_copy(t, m, sems.at[n]) for n, (t, m) in enumerate(zip(tables, scalars))
    ]
    for c in copies:
        c.start()
    return copies


def padded_copy(source, target, sem):
    return pltpu.make_async_copy(source, target.at[pl.ds(LEAD * 8, ROWS * 8)], sem)


def cover(pair, planes):
    lane = iota((8, LANES), 1)
    sub = iota((8, LANES), 0)

    def body(p, carry):
        off = pair(p, 3)
        rows = window(planes, off >> 7)
        counts = [rows[rows_at(8 * i, COUNT), :] for i in range(GROUPS)]
        for i in range(GROUPS):
            s = (sub + 8 * i) * LANES + lane - (off & 127)
            inside = (s >= 0) & (s < SLAB)
            rows[rows_at(8 * i, COUNT), :] = counts[i] + jnp.where(inside, 1.0, 0.0)
        return carry

    lax.fori_loop(0, live_count(pair), body, 0)


def early_kernel(
    column, near, image, far_in,
    cross, weight_out, value_out, own_out, side_out, count_out,
    far, planes, scalars, sems,
):
    reads = scalar_copies((column,), (scalars,), sems)
    copy = padded_copy(far_in, far, sems.at[1])
    copy.start()
    clear_ends(far)
    clear((planes,))
    here = Here()

    def rows(g, carry):
        w = jnp.zeros((8, LANES), jnp.float32)
        v = jnp.zeros((8, LANES), jnp.float32)
        for z in range(DEPTH):
            slope = near[pl.ds(64 * g + (LEAD * 8 + z), 8, stride=8), :]
            w = w + slope * slope
            v = v + slope * image[pl.ds(64 * g + (LEAD * 8 + z), 8, stride=8), :]
        at = pl.ds(pl.multiple_of(8 * g, 8), 8)
        weight_out[at, :] = w
        value_out[at, :] = v
        return carry

    lax.fori_loop(0, ROWS // 8, rows, 0)
    reads[0].wait()
    cover(sent_reader(scalars, 1), planes)
    slabs(sent_reader(scalars, 1), 0, near, near, image, cross, planes, 0, False)
    copy.wait()
    slabs(sent_reader(scalars, here.to_a), CAP, far, near, image, cross, planes, 2, False)
    own_out[...] = collected(planes, 0)
    side_out[...] = collected(planes, 2)
    count_out[...] = planes[all_rows(COUNT), :]


def late_kernel(
    blocks, shifts, column, side_a, side_b,
    near, image, cross_early, weight, value, own, side, counted, far_in,
    cross, weight_out, part_out,
    far, planes, scalars_own, scalars_a, scalars_b, sems, scalar_sems,
):
    reads = scalar_copies(
        (column, side_a, side_b), (scalars_own, scalars_a, scalars_b), scalar_sems
    )
    copy = padded_copy(far_in, far, sems.at[0])
    copy.start()
    here = Here(blocks, shifts)
    clear_ends(far)
    clear((planes,))
    spline = Spline()
    field = spline.field(local_values(here, (column, side_a, side_b))) + here.rigid
    planes[all_rows(FIELD), :] = field
    for c in reads:
        c.wait()
    cover(sent_reader(scalars_a, 2 - here.to_a), planes)
    cover(sent_reader(scalars_b, 2 - here.to_b), planes)
    slab_steps(
        [
            (sent_reader(scalars_own, 1), 0, cross_early, 0),
            (sent_reader(scalars_own, here.to_a), CAP, cross_early, 2),
        ],
        planes,
    )
    copy.wait()
    slabs(sent_reader(scalars_own, here.to_b), 0, far, near, image, cross, planes, 4, True)
    n = counted[...] + planes[all_rows(COUNT), :]
    w = weight[...] * n
    weight_out[...] = w
    mine = value[...] * n + w * planes[all_rows(FIELD), :] - own[...] - collected(planes, 0)
    others = [side[...] + collected(planes, 2), collected(planes, 4)]
    rows = spline.adjoints([mine] + others, w)
    part_out[0:1, :] = rows[0]
    part_out[1:2, :] = -rows[1]
    part_out[2:3, :] = -rows[2]
    part_out[3:4, :] = here.block_row()
    for m in range(4):
        part_out[4 + m : 5 + m, :] = rows[3 + m]


def near_tiles(both, ahead, third, behind):
    me, a = both[0:8, :], both[8:16, :]
    d, b = ahead[0:8, :], ahead[8:16, :]
    sd, sb = behind[0:8, :], behind[8:16, :]
    c = third[0:8, :]
    return [
        (me, me[0:1] + a[1:2] + b[2:3]),
        (a, a[0:1] + me[1:2] + sb[2:3]),
        (b, b[0:1] + d[1:2] + me[2:3]),
        (d, d[0:1] + b[1:2] + c[2:3]),
        (sb, sb[0:1] + sd[1:2] + a[2:3]),
    ]


def folded(rows):
    return rows + pltpu.roll(rows, BLOCK, 1)


def block_sums(tiles, block):
    total = jnp.zeros((1, LANES), jnp.float32)
    for ref, grad in tiles:
        total = total + jnp.where(ref[3:4] == block, grad, 0.0)
    lane = iota((1, LANES), 1)
    return jnp.where(lane < BLOCK, folded(total), 0.0)


def pulled(coef):
    lane = iota((1, LANES), 1)
    y = coef - 2.0 * pltpu.roll(coef, LANES - 1, 1) + pltpu.roll(coef, LANES - 2, 1)
    y = jnp.where(lane < BLOCK - 2, y, 0.0)
    return jnp.where(lane < BLOCK, y - 2.0 * pltpu.roll(y, 1, 1) + pltpu.roll(y, 2, 1), 0.0)


def solve(target, factor, steps):
    y = []
    for i in range(BLOCK):
        v = target[i : i + 1, :]
        for j in range(1, 4):
            if i >= j:
                v = v - factor[j * BLOCK + i - j : j * BLOCK + i - j + 1, :] * y[i - j]
        y.append(v)
    x = [None] * BLOCK
    for i in reversed(range(BLOCK)):
        v = y[i] * factor[i : i + 1, :]
        for j in range(3, 0, -1):
            if i + j < BLOCK:
                v = v - factor[j * BLOCK + i : j * BLOCK + i + 1, :] * x[i + j]
        x[i] = v
        steps[i : i + 1, :] = v


def across(rows):
    block = jnp.concatenate(rows + [jnp.zeros((LANES - len(rows), LANES), jnp.float32)], axis=0)
    return block.T


def joined(coefs):
    lane = iota((1, LANES), 1)
    return jnp.where(lane < BLOCK, coefs[0], pltpu.roll(coefs[1], BLOCK, 1))


def step_kernel(
    blocks, both, ahead, third, behind, column, side_a, side_b, start, weight,
    cross_early, cross_late,
    part_out, state, factor,
    planes, steps, work, scalars, scalar_sems,
):
    reads = scalar_copies((column,), (scalars,), scalar_sems)
    here = Here(blocks)
    clear((planes, steps))
    lane = iota((1, LANES), 1)
    zero = jnp.zeros((1, LANES), jnp.float32)
    tiles = near_tiles(both, ahead, third, behind)
    knots = local_values(here, (column, side_a, side_b))
    coefs = [
        jnp.where(lane < BLOCK, knots, 0.0),
        jnp.where(lane < BLOCK, pltpu.roll(knots, BLOCK, 1), 0.0),
        jnp.concatenate([start[...], jnp.zeros((1, LANES - BLOCK), jnp.float32)], axis=1),
    ]
    sums = []
    rows = []
    for q, block in enumerate(here.block_ids()):
        gradsum = block_sums(tiles, block)
        sums.append(gradsum)
        bands = []
        for m in range(4):
            total = zero
            for ref, _ in tiles:
                total = total + jnp.where(ref[3:4] == block, ref[4 + m : 5 + m], 0.0)
            total = jnp.where((lane & (BLOCK - 1)) + m < BLOCK, total, 0.0)
            bands.append(folded(total))
        inside = lambda cond: jnp.where(cond, 1.0, 0.0)
        upper, lower = inside(lane < BLOCK - 2), inside(lane >= 2)
        middle = inside((lane >= 1) & (lane < BLOCK - 1))
        bands[0] = bands[0] + smooth_weight * (upper + 4.0 * middle + lower) + ridge_weight
        bands[1] = bands[1] - smooth_weight * 2.0 * (
            upper + inside((lane >= 1) & (lane < BLOCK - 1))
        )
        bands[2] = bands[2] + smooth_weight * upper
        target = -(gradsum + smooth_weight * pulled(coefs[q]))
        rows += bands + [target, zero, zero, zero]
    work[...] = across(rows)
    turned = [work[0:BLOCK, :]] + [pltpu.roll(work[0:BLOCK, :], LANES - m, 1) for m in range(1, 5)]
    band = [[turned[m][i : i + 1, :] for i in range(BLOCK)] for m in range(4)]
    for i in range(BLOCK):
        r = 1.0 / band[0][i]
        factor[i : i + 1, :] = r
        cs = [band[m][i] for m in range(1, 4)]
        ls = [v * r for v in cs]
        for j in range(1, 4):
            factor[j * BLOCK + i : j * BLOCK + i + 1, :] = ls[j - 1]
            if i + j < BLOCK:
                for m in range(0, 4 - j):
                    band[m][i + j] = band[m][i + j] - ls[j - 1] * cs[j - 1 + m]
    solve(turned[4], factor, steps)
    moved = steps[...].T
    change = [moved[8 * q : 8 * q + 1, :] for q in range(3)]
    state[...] = jnp.concatenate(
        [coefs[q] + change[q] for q in range(3)] + [zero] + sums + [zero], axis=0
    )
    spline = Spline()
    planes[all_rows(FIELD), :] = spline.field(joined(change))
    reads[0].wait()
    slab_steps(
        [
            (sent_reader(scalars, 1), 0, cross_early, 0),
            (sent_reader(scalars, here.to_a), CAP, cross_early, 2),
            (sent_reader(scalars, here.to_b), 0, cross_late, 4),
        ],
        planes,
    )
    mine = weight[...] * planes[all_rows(FIELD), :] - collected(planes, 0)
    rows = spline.adjoints([mine, collected(planes, 2), collected(planes, 4)])
    part_out[0:1, :] = rows[0]
    part_out[1:2, :] = -rows[1]
    part_out[2:3, :] = -rows[2]
    part_out[3:4, :] = here.block_row()
    part_out[4:8, :] = jnp.zeros((4, LANES), jnp.float32)


CHUNKS = 8


def final_kernel(
    blocks, shifts, both, ahead, third, behind, state, factor, grad, image,
    coef_out, warped_out,
    moved_image, field, steps, out_sems,
):
    size = ROWS * 8 // CHUNKS
    at = [pl.ds(n * size, size) for n in range(CHUNKS)]
    here = Here(blocks, shifts)
    steps[...] = jnp.zeros((LANES, LANES), jnp.float32)
    tiles = near_tiles(both, ahead, third, behind)
    zero = jnp.zeros((1, LANES), jnp.float32)
    coefs = [state[q : q + 1, :] for q in range(3)]
    rows = []
    for q, block in enumerate(here.block_ids()):
        gradsum = state[4 + q : 5 + q, :] + block_sums(tiles, block)
        rows += [-(gradsum + smooth_weight * pulled(coefs[q]))] + [zero] * 7
    solve(across(rows)[0:BLOCK, :], factor, steps)
    moved = steps[...].T
    coefs = [coefs[q] + moved[8 * q : 8 * q + 1, :] for q in range(3)]
    coef_out[...] = coefs[2][:, :BLOCK]
    spline = Spline()
    field[...] = spline.field(joined(coefs)) + here.rigid
    stores = []
    for n in range(CHUNKS):

        def body(g, carry):
            for r in range(8):
                row = g * 8 + r
                rows = pl.ds(pl.multiple_of(row * 8, 8), 8)
                moved_image[rows, :] = image[rows, :] + grad[rows, :] * field[pl.ds(row, 1), :]
            return carry

        lax.fori_loop(n * size // 64, (n + 1) * size // 64, body, 0)
        stores.append(pltpu.make_async_copy(moved_image.at[at[n]], warped_out.at[at[n]], out_sems.at[n]))
        stores[-1].start()
    for copy in stores:
        copy.wait()


VMEM = pl.BlockSpec(memory_space=pltpu.VMEM)
ANY = pl.BlockSpec(memory_space=pl.ANY)
HBM = pl.BlockSpec(memory_space=pltpu.HBM)


def f32(*shape):
    return jax.ShapeDtypeStruct(shape, jnp.float32)


def call(kernel, name, in_specs, out_specs, out_shape, scratch):
    return pl.pallas_call(
        kernel,
        name=name,
        in_specs=in_specs,
        out_specs=out_specs,
        out_shape=out_shape,
        scratch_shapes=scratch,
        compiler_params=pltpu.CompilerParams(vmem_limit_bytes=24 * 1024 * 1024),
    )


def whole():
    return pltpu.VMEM((PADDED * 8, LANES), jnp.float32)


def square():
    return pltpu.VMEM((LANES, LANES), jnp.float32)


def viewed(block):
    return block.reshape(DEPTH, ROWS, LANES).transpose(1, 0, 2).reshape(ROWS * DEPTH, LANES)


def per_device(images, gradient, shifts, tile_blocks, intersections, start_coefficients):
    tiles = lax.axis_size("tile")
    knots = lax.axis_size("knot")
    ids = range(tiles)
    swap_a = [(i, i ^ 1) for i in ids]
    swap_b = [(i, ((i - 1) ^ 1) + 1) for i in ids if 0 < i < tiles - 1]
    swap_c = [(i, i + 3 if i % 2 else i - 3) for i in ids]
    swap_c = [(i, j) for i, j in swap_c if 0 <= j < tiles]
    same_d = [(i, i + 2 if i % 2 == 0 else i - 2) for i in ids]
    same_d = [(i, j) for i, j in same_d if 0 <= j < tiles]

    def move(value, route):
        return lax.ppermute(value, "tile", route)

    def over_knot(value):
        return [value] + [
            lax.ppermute(value, "knot", [(i, (i + s) % knots) for i in range(knots)])
            for s in range(1, knots)
        ]

    shifts = shifts.reshape(1, 1)
    far_b = move(gradient, swap_b)
    far_a = move(gradient, swap_a)
    sent = jnp.pad(intersections.reshape(1, -1).astype(jnp.float32), ((0, 0), (0, 8)))
    column = jnp.concatenate(over_knot(start_coefficients) + [sent.reshape(2, BLOCK)], axis=0)
    side_a, side_b = move(column, swap_a), move(column, swap_b)

    grad, image = viewed(gradient), viewed(images)
    ends = ((LEAD * 8, (PADDED - LEAD - ROWS) * 8), (0, 0))
    near, held = jnp.pad(grad, ends), jnp.pad(image, ends)
    cross_early, *sums = call(
        early_kernel, "early_pairs",
        [VMEM] * 3 + [HBM],
        [VMEM] * 6,
        [f32(2 * CAP, SLAB_ROWS, LANES)] + [f32(ROWS, LANES)] * 5,
        [whole()] * 2 + [pltpu.SMEM((6, BLOCK), jnp.float32), pltpu.SemaphoreType.DMA((2,))],
    )(column, near, held, viewed(far_a))
    cross_late, weight, part = call(
        late_kernel, "late_pairs",
        [VMEM] * 13 + [ANY],
        [VMEM] * 3,
        [f32(CAP, SLAB_ROWS, LANES), f32(ROWS, LANES), f32(8, LANES)],
        [whole()] * 2
        + [pltpu.SMEM((6, BLOCK), jnp.float32)] * 3
        + [pltpu.SemaphoreType.DMA((1,)), pltpu.SemaphoreType.DMA((3,))],
    )(
        tile_blocks, shifts, column, side_a, side_b, near, held, cross_early, *sums,
        viewed(far_b),
    )

    def exchange(value):
        v = over_knot(value)
        me = (v[0] + v[1]) + (v[2] + v[3])
        third = move(jnp.pad(me, ((0, 24), (0, 0))), swap_c)
        both = jnp.concatenate([me, move(me, swap_a)], axis=0)
        ahead = move(both, same_d)
        third, ahead = lax.optimization_barrier((third, ahead))
        return both, ahead, third, move(ahead, swap_a)

    part, state, factor = call(
        step_kernel, "first_step",
        [VMEM] * 12,
        [VMEM] * 3,
        [f32(8, LANES), f32(8, LANES), f32(4 * BLOCK, LANES)],
        [whole(), square(), square()]
        + [pltpu.SMEM((6, BLOCK), jnp.float32), pltpu.SemaphoreType.DMA((1,))],
    )(
        tile_blocks, *exchange(part), column, side_a, side_b, start_coefficients, weight,
        cross_early, cross_late,
    )
    coef, warped = call(
        final_kernel, "second_step",
        [VMEM] * 10,
        [VMEM, ANY],
        [f32(1, BLOCK), f32(ROWS * DEPTH, LANES)],
        [pltpu.VMEM((ROWS * DEPTH, LANES), jnp.float32)]
        + [pltpu.VMEM((ROWS, LANES), jnp.float32), square()]
        + [pltpu.SemaphoreType.DMA((CHUNKS,))],
    )(tile_blocks, shifts, *exchange(part), state, factor, grad, image)
    warped = warped.reshape(ROWS, DEPTH, LANES).transpose(1, 0, 2).reshape(1, DEPTH, ROWS * LANES)
    return coef, warped


def solution(mesh):
    placed = (
        P("tile", "knot", None),
        P("tile", "knot", None),
        P("tile"),
        P("tile", None),
        P("tile", None, None, None),
        P(("tile", "knot"), None),
    )
    return jax.shard_map(
        per_device,
        mesh=mesh,
        in_specs=placed,
        out_specs=(P(("tile", "knot"), None), P("tile", "knot", None)),
        check_vma=False,
    )
```
